128 devices in a mesh: grp: 16 (over z, y_lo, core), dp: 8 (over x, y_hi).
Axes of the slice: x: 4, y: 4 (y_hi: 2, y_lo: 2; y = y_hi * 2 + y_lo), z: 4, core: 2. Of those that a mesh axis runs over, the one named last changes fastest.
Arguments:
- w_qkv: bfloat16 [8192, 768], P('dp'), may hold values from -0.0625 to 0.0625
- qkv_bias: float32 [768], replicated, may hold values from -3 to 3
- w_out: bfloat16 [512, 8192], P('dp'), may hold values from -0.25 to 0.25
- video_x: bfloat16 [8, 2048, 8192], P('dp', 'grp'), may hold values from -30 to 30
- video_pos: int32 [3, 8, 2048], P(None, 'dp', 'grp'), may hold values from 0 to 511
- short_x: bfloat16 [128, 256, 8192], P(('dp', 'grp')), may hold values from -30 to 30
- short_pos: int32 [3, 128, 256], P(None, ('dp', 'grp')), may hold values from 0 to 511
- short_seg: int32 [128, 256], P(('dp', 'grp')), may hold values from 0 to 31, never falling along the last dimension, each value on 1 to 128 neighbouring positions
- video_cot: bfloat16 [8, 2048, 8192], P('dp', 'grp'), may hold values from -0.0390625 to 0.0390625
- short_cot: bfloat16 [128, 256, 8192], P(('dp', 'grp')), may hold values from -0.109375 to 0.109375
Outputs:
- video_y: bfloat16 [8, 2048, 8192], P('dp', 'grp')
- short_y: bfloat16 [128, 256, 8192], P(('dp', 'grp'))
- grad_qkv: float32 [8192, 768], P(('grp', 'dp'))
- grad_out: float32 [512, 8192], P(None, ('grp', 'dp'))
- grad_bias: float32 [768], replicated
The draws below stay inside these ranges and needn't reach their ends.
Inputs may be any that keep to these rules, and one draw needn't show every extreme that they name: `short_seg`: within each block of 256 rows the sample numbers never fall, and each sample holds 1 to 128 rows.
All inputs are finite; a program needn't handle non-finite values.
Results may differ from the reference program's by a relative error of at most 0.035.
Values may be sent and summed in bfloat16 or wider, within the bound.
No kernel may reach another device: no remote copies, remote signals or barrier semaphores. Data moves between devices by JAX's collectives and lax.ppermute only.
A program may use at most 128 MiB of HBM per device.

```python
import math
import jax
import jax.numpy as jnp
import numpy as np
from jax import lax

D = 8192
HEAD = 128
QH = 4
LONG_DEV = 128
SHORT_DEV = 256
VIDEOS = 8
VLEN = 2048
NSHORT = 128
N_GRP = 16
N_DP = 8


def drawn_rows(rand_key, shape):
    return jnp.clip(jax.random.normal(rand_key, shape, jnp.float32), -6.0, 6.0)


def block_boost(rand_key, row_blocks, block_rows):
    pair_key = jax.random.fold_in(rand_key, 5)
    pairing = jax.random.permutation(pair_key, row_blocks).astype(jnp.int32)
    row_block = jnp.arange(row_blocks * block_rows, dtype=jnp.int32) // block_rows
    column_block = jnp.arange(D, dtype=jnp.int32) // (D // row_blocks)
    hit = pairing[row_block][:, None] == column_block[None, :]
    return jnp.where(hit, 4.0, 1.0)


def draw_video_x(key, part):
    key = jax.random.fold_in(key, 11)
    row_blocks = VIDEOS * (VLEN // LONG_DEV)
    factor = block_boost(key, row_blocks, LONG_DEV).reshape(VIDEOS, VLEN, D)
    values = drawn_rows(key, (VIDEOS, VLEN, D))
    return (values * factor).astype(jnp.bfloat16)


def draw_short_x(key, part):
    key = jax.random.fold_in(key, 23)
    return drawn_rows(key, (NSHORT, SHORT_DEV, D)).astype(jnp.bfloat16)


def plant(result, key, smallest, top_value):
    longest = result.shape.index(max(result.shape))
    spots = []
    for shift in (0, 1):
        where = [jax.random.randint(jax.random.fold_in(key, axis), (), 0, length) for axis, length in enumerate(result.shape)]
        where[longest] = (where[longest] + shift) % result.shape[longest]
        spots.append(tuple(where))
    return result.at[spots[0]].set(smallest).at[spots[1]].set(top_value)


def strengthened(entries, own_key, source, target, shards_of, factor):
    owner, partner = [(jnp.arange(entries.shape[dim]) // (entries.shape[dim] // shards_of)).reshape([-1 if axis == dim else 1 for axis in range(entries.ndim)]) for dim in (source, target)]
    chosen = jax.random.permutation(own_key, shards_of)[partner]
    strong = (owner == chosen) | (owner == (partner + shards_of // 2) % shards_of)
    return jnp.where(strong, factor * entries, entries)


def levels(rng, shape, cuts, low, top_value):
    level = 1.0
    for dim, blocks in cuts:
        draws = jax.random.uniform(jax.random.fold_in(jax.random.fold_in(rng, 6), dim), (blocks,), jnp.float32, low / len(cuts), top_value / len(cuts))
        level = level * jnp.repeat(jnp.exp(draws), shape[dim] // blocks).reshape((-1,) + (1,) * (len(shape) - 1 - dim))
    return level


def profile(number_of, total, most, skew):
    loads = [(1 << 20) // math.isqrt(rank ** skew) + 1 for rank in range(2, number_of + 1)]
    surplus, holding = total - most - (number_of - 1), [1] * (number_of - 1)
    while surplus > 0:
        movable = [i for i in range(number_of - 1) if holding[i] < most]
        mass, budget = sum([loads[i] for i in movable]), surplus
        for i in movable:
            more = min(most - holding[i], max(1, budget * loads[i] // mass), surplus)
            holding[i] = holding[i] + more
            surplus = surplus - more
    return np.array([most] + holding)


def ragged(rng, amount, total, bound, lean):
    if amount == 2:
        one = jax.random.randint(rng, (), max(1, total - bound), min(bound, total - 1) + 1)
        return jnp.stack([one, total - one])
    tallies = jnp.asarray(profile(amount, total, bound, lean), jnp.int32)
    twos = (amount - 1) // 2
    giver, sink = tallies[1:1 + 2 * twos:2], tallies[2:2 + 2 * twos:2]
    margin = jnp.minimum(giver - 1, bound - sink)
    moved = jax.random.randint(jax.random.fold_in(rng, 1), (twos,), 0, 1 << 20) % (margin + 1)
    tallies = tallies.at[1:1 + 2 * twos:2].set(giver - moved).at[2:2 + 2 * twos:2].set(sink + moved)
    return tallies[jax.random.permutation(jax.random.fold_in(rng, 2), amount)]


def noise(stream_key, extent, scale, most, cuts=(), kind=jnp.bfloat16):
    gain = levels(stream_key, extent, cuts, -0.22, 0.18) if cuts else 1.0
    array = jax.random.normal(stream_key, extent, jnp.float32) * scale * gain
    return jnp.minimum(jnp.maximum(array, -most), most).astype(kind)


def gaussian_with(stream_key, extent, scale, bound, pieces, heavy, kind=jnp.bfloat16):
    values = scale * jax.random.normal(stream_key, extent, jnp.float32)
    if pieces:
        values = values * levels(stream_key, extent, pieces, -0.22, 0.18)
    return jnp.clip(strengthened(values, jax.random.fold_in(stream_key, 3), *heavy), -bound, bound).astype(kind)


def setup_inputs(seed: int = 0) -> dict:
    streams_of = jax.random.split(jax.random.key(seed), 11)
    return {
        "w_qkv": noise(streams_of[0], (D, (QH + 2) * HEAD), D ** -0.5, 0.0625, ((0, 8),)),
        "qkv_bias": noise(streams_of[1], ((QH + 2) * HEAD,), 0.5, 3.0, (), jnp.float32),
        "w_out": noise(streams_of[2], (QH * HEAD, D), (QH * HEAD) ** -0.5, 0.25, ((0, 8),)),
        "video_x": draw_video_x(jax.random.fold_in(streams_of[10], 71), 0),
        "video_pos": plant(jax.random.randint(streams_of[4], (3, VIDEOS, VLEN), 0, 512), jax.random.fold_in(streams_of[4], 1), 0, 511).astype(jnp.int32),
        "short_x": draw_short_x(jax.random.fold_in(streams_of[10], 71), 0),
        "short_pos": plant(jax.random.randint(streams_of[6], (3, NSHORT, SHORT_DEV), 0, 512), jax.random.fold_in(streams_of[6], 1), 0, 511).astype(jnp.int32),
        "short_seg": jax.vmap(lambda own: jnp.searchsorted(jnp.cumsum(ragged(own, max(SHORT_DEV // 8, 3), SHORT_DEV, SHORT_DEV // 2, 2)), jnp.arange(SHORT_DEV), side="right"))(jax.random.split(streams_of[7], NSHORT)).reshape((NSHORT, SHORT_DEV)).astype(jnp.int32),
        "video_cot": gaussian_with(streams_of[8], (VIDEOS, VLEN, D), ((N_GRP * N_DP * (LONG_DEV + SHORT_DEV)) ** -0.5), 0.0390625, ((0, 8), (1, 16)), (1, 2, 16, 2.0)),
        "short_cot": gaussian_with(streams_of[9], (NSHORT, SHORT_DEV, D), ((N_GRP * N_DP * (LONG_DEV + SHORT_DEV)) ** -0.5), 0.109375, ((0, 128),), (0, 2, 128, 5.5)),
    }


theta_log = 13.815510557964274


def rope_angles(positions):
    half_dim = HEAD // 2
    freq_index = jnp.arange(half_dim, dtype=jnp.int32)
    inv_freq = jnp.exp(freq_index.astype(jnp.float32) * (-2.0 * theta_log / HEAD))
    first_cut = HEAD // 8
    second_cut = first_cut + 3 * HEAD // 16
    pos_float = positions.astype(jnp.float32)
    chosen_pos = jnp.where((freq_index < first_cut)[None, :], pos_float[0][:, None],
                           jnp.where((freq_index < second_cut)[None, :], pos_float[1][:, None], pos_float[2][:, None]))
    angles = chosen_pos * inv_freq[None, :]
    return jnp.cos(angles), jnp.sin(angles)


def rotate(tensor, cosines, sine_vals, direction):
    half_dim = HEAD // 2
    wide_cos = cosines[:, None, :]
    wide_sin = sine_vals[:, None, :] * direction
    front_half = tensor[..., :half_dim]
    back_half = tensor[..., half_dim:]
    return jnp.concatenate([front_half * wide_cos - back_half * wide_sin,
                            back_half * wide_cos + front_half * wide_sin], axis=-1)


def attend(queries, keys_in, values_in, allowed):
    scores = jnp.einsum('rhe,ke->rhk', queries.astype(jnp.float32), keys_in.astype(jnp.float32)) * HEAD ** -0.5
    scores = jnp.where(allowed, scores, -1e30)
    peak_score = jnp.max(scores, axis=-1, keepdims=True)
    weights = jnp.where(allowed, jnp.exp(scores - peak_score), 0.0)
    weight_sum = jnp.sum(weights, axis=-1, keepdims=True)
    probs = weights / weight_sum
    probs_half = probs.astype(jnp.bfloat16)
    attended = jnp.einsum('rhk,ke->rhe', probs_half.astype(jnp.float32), values_in.astype(jnp.float32)).astype(jnp.bfloat16)
    return attended, probs, probs_half


def run_block(tokens, positions, cotangent, allowed, w_qkv, qkv_bias, w_out):
    row_count = tokens.shape[0]
    att_width = QH * HEAD
    projected = jnp.dot(tokens, w_qkv, preferred_element_type=jnp.float32) + qkv_bias[None, :]
    cosines, sine_vals = rope_angles(positions)
    queries = rotate(projected[:, :att_width].reshape(row_count, QH, HEAD), cosines, sine_vals, 1.0).astype(jnp.bfloat16)
    key_rows = rotate(projected[:, att_width:att_width + HEAD].reshape(row_count, 1, HEAD), cosines, sine_vals, 1.0)[:, 0].astype(jnp.bfloat16)
    value_rows = projected[:, att_width + HEAD:].astype(jnp.bfloat16)
    attended, probs, probs_half = attend(queries, key_rows, value_rows, allowed)
    flat_out = attended.reshape(row_count, att_width)
    layer_out = jnp.dot(flat_out, w_out, preferred_element_type=jnp.float32).astype(jnp.bfloat16)
    grad_attended = lax.dot_general(cotangent, w_out, (((1,), (1,)), ((), ())),
                                    preferred_element_type=jnp.float32).astype(jnp.bfloat16)
    grad_heads = grad_attended.reshape(row_count, QH, HEAD).astype(jnp.float32)
    deltas = jnp.sum(grad_heads * attended.astype(jnp.float32), axis=-1)
    grad_probs = jnp.einsum('rhe,ke->rhk', grad_heads, value_rows.astype(jnp.float32))
    grad_scores = (probs * (grad_probs - deltas[..., None]) * HEAD ** -0.5).astype(jnp.bfloat16).astype(jnp.float32)
    grad_queries = jnp.einsum('rhk,ke->rhe', grad_scores, key_rows.astype(jnp.float32))
    grad_keys = jnp.einsum('rhk,rhe->ke', grad_scores, queries.astype(jnp.float32))
    grad_values = jnp.einsum('rhk,rhe->ke', probs_half.astype(jnp.float32), grad_heads)
    grad_queries = rotate(grad_queries, cosines, sine_vals, -1.0).reshape(row_count, att_width)
    grad_keys = rotate(grad_keys[:, None, :], cosines, sine_vals, -1.0)[:, 0]
    grad_projected = jnp.concatenate([grad_queries, grad_keys, grad_values], axis=1)
    return layer_out, flat_out, grad_projected.astype(jnp.bfloat16), jnp.sum(grad_projected, axis=0)


def reference(w_qkv, qkv_bias, w_out, video_x, video_pos, short_x, short_pos, short_seg, video_cot, short_cot):
    position = jnp.arange(VLEN, dtype=jnp.int32)
    video_allowed = (position[None, :] <= position[:, None])[:, None, :]

    def video_one(members):
        tokens, positions, cotangent = members
        return run_block(tokens, positions, cotangent, video_allowed, w_qkv, qkv_bias, w_out)

    video_y, video_flat, video_grad, video_bias = lax.map(video_one, (video_x, jnp.moveaxis(video_pos, 1, 0), video_cot))
    short_spot = jnp.arange(SHORT_DEV, dtype=jnp.int32)

    def short_one(members):
        tokens, positions, segment, cotangent = members
        allowed = ((segment[None, :] == segment[:, None]) & (short_spot[None, :] <= short_spot[:, None]))[:, None, :]
        return run_block(tokens, positions, cotangent, allowed, w_qkv, qkv_bias, w_out)

    short_y, short_flat, short_grad, short_bias = lax.map(short_one, (short_x, jnp.moveaxis(short_pos, 1, 0), short_seg, short_cot))
    groups = NSHORT
    row_total = LONG_DEV + SHORT_DEV

    def stack_rows(video_part, short_part):
        width_last = video_part.shape[-1]
        joined = jnp.concatenate([video_part.reshape(VIDEOS, NSHORT // VIDEOS, LONG_DEV, width_last),
                                  short_part.reshape(VIDEOS, NSHORT // VIDEOS, SHORT_DEV, width_last)], axis=2)
        return joined.reshape(groups, row_total, width_last)

    dev_tokens = stack_rows(video_x, short_x)
    dev_grads = stack_rows(video_grad, short_grad)
    dev_flat = stack_rows(video_flat, short_flat)
    dev_cot = stack_rows(video_cot, short_cot)

    def add_term(carried, dev_item):
        tokens, grad_rows, flat_out, cotangent = dev_item
        term_proj = lax.dot_general(tokens, grad_rows, (((0,), (0,)), ((), ())), preferred_element_type=jnp.float32)
        term_proj = lax.optimization_barrier(term_proj.astype(jnp.bfloat16)).astype(jnp.float32)
        term_output = lax.dot_general(flat_out, cotangent, (((0,), (0,)), ((), ())), preferred_element_type=jnp.float32)
        term_output = lax.optimization_barrier(term_output.astype(jnp.bfloat16)).astype(jnp.float32)
        return (carried[0] + term_proj, carried[1] + term_output), None

    start_sums = (jnp.zeros((D, (QH + 2) * HEAD), jnp.float32), jnp.zeros((QH * HEAD, D), jnp.float32))
    (grad_qkv, grad_out), _ = lax.scan(add_term, start_sums, (dev_tokens, dev_grads, dev_flat, dev_cot))
    grad_bias = jnp.sum(video_bias, axis=0) + jnp.sum(short_bias, axis=0)
    return video_y, short_y, grad_qkv, grad_out, grad_bias
```

```python
import functools

import jax
import jax.numpy as jnp
from jax import lax
from jax.experimental import pallas as pl
from jax.experimental.pallas import tpu as pltpu
from jax.sharding import Mesh
from jax.sharding import PartitionSpec as P

HEAD = 128
QH = 4
ATT = QH * HEAD
AXES = ("z", "yl", "c", "x", "yh")
SIZES = (4, 2, 2, 4, 2)
GRP = ("z", "yl", "c")
DP = ("x", "yh")
BF = jnp.bfloat16
F32 = jnp.float32
THETA_LOG = 13.815510557964274


def device_index(z, y, c, x):
    z, y, c, x = z % 4, y % 4, c % 2, x % 4
    return (((z * 2 + y % 2) * 2 + c) * 4 + x) * 2 + y // 2


def pairs(target):
    result = []
    for z in range(4):
        for y in range(4):
            for c in range(2):
                for x in range(4):
                    result.append((device_index(z, y, c, x), device_index(*target(z, y, c, x))))
    return result


def move(value, target):
    return lax.ppermute(value, AXES, pairs(target))


def other_core(value):
    return move(value, lambda z, y, c, x: (z, y, c + 1, x))


def to_x(value, step):
    return move(value, lambda z, y, c, x: (z, y, c, x + step))


def to_z(value, step):
    return move(value, lambda z, y, c, x: (z + step, y, c, x))


def to_y(value, step):
    return move(value, lambda z, y, c, x: (z, y + step, c, x))


def across(value):
    return move(value, lambda z, y, c, x: (z, 3 - y, c, x))


def to_first(value, step):
    return move(
        value, lambda z, y, c, x: (z + step, y, c, x) if c == 0 else (z, y, c, x + step)
    )


def to_second(value, step):
    return move(
        value, lambda z, y, c, x: (z, y, c, x + step) if c == 0 else (z + step, y, c, x)
    )


def params(limit=48):
    return pltpu.CompilerParams(vmem_limit_bytes=limit * 1024 * 1024)


def halves_kernel(core_ref, a0, b0, a1, b1, mine, theirs):
    n = a0.shape[0]
    first = core_ref[0] == 0

    @pl.when(first)
    def _():
        mine[:n] = a0[...]
        mine[n:] = b0[...]
        theirs[:n] = a1[...]
        theirs[n:] = b1[...]

    @pl.when(jnp.logical_not(first))
    def _():
        mine[:n] = a1[...]
        mine[n:] = b1[...]
        theirs[:n] = a0[...]
        theirs[n:] = b0[...]


def column_halves(core, video, short):
    rows = video.shape[0] + short.shape[0]
    spec = lambda n, k: pl.BlockSpec((n, 512), lambda j, s: (0, 2 * j + k))
    out = pl.BlockSpec((rows, 512), lambda j, s: (0, j))
    shape = jax.ShapeDtypeStruct((rows, 4096), BF)
    nv, ns = video.shape[0], short.shape[0]
    return pl.pallas_call(
        halves_kernel,
        grid_spec=pltpu.PrefetchScalarGridSpec(
            num_scalar_prefetch=1,
            grid=(8,),
            in_specs=[spec(nv, 0), spec(ns, 0), spec(nv, 1), spec(ns, 1)],
            out_specs=[out, out],
        ),
        out_shape=[shape, shape],
        compiler_params=params(),
        name="column_halves",
    )(core, video, short, video, short)


def weight_half_kernel(core_ref, block, result):
    result[0] = block[...]


def weight_half(core, w):
    return pl.pallas_call(
        weight_half_kernel,
        grid_spec=pltpu.PrefetchScalarGridSpec(
            num_scalar_prefetch=1,
            grid=(8,),
            in_specs=[pl.BlockSpec((64, 512), lambda j, s: (0, 2 * j + s[0]))],
            out_specs=pl.BlockSpec((1, 64, 512), lambda j, s: (j, 0, 0)),
        ),
        out_shape=jax.ShapeDtypeStruct((8, 64, 512), BF),
        compiler_params=params(),
        name="weight_half",
    )(core, w)


def put(buffer, piece, *index):
    index = tuple(index) + (0,) * (buffer.ndim - len(index))
    return lax.dynamic_update_slice(buffer, piece, index)


def ring(pair, mover, position):
    got = [(position, pair)]
    for step in (1, 3, 2):
        got.append(((position + 4 - step) % 4, mover(pair, step)))
    return got


def gather(lower, upper, at):
    m, n = lower.shape[1:]
    x, yh, z = at["x"], at["yh"], at["z"]
    whole = jnp.zeros((4, 2, 8, m, n), BF)
    quarter = lax.dynamic_slice(upper, (z, 0, 0), (1, m, n))
    pair_q = jnp.stack([quarter, across(quarter)])
    pair_l = jnp.stack([lower, across(lower)])
    block = jnp.zeros((4, 2, 1, m, n), BF)
    for place, pair in ring(pair_q, to_x, x):
        block = put(block, pair[0][None, None], place, yh)
        block = put(block, pair[1][None, None], place, 1 - yh)
    for place, pair in ring(pair_l, to_x, x):
        whole = put(whole, pair[0][None, None], place, yh)
        whole = put(whole, pair[1][None, None], place, 1 - yh)
    for place, got in ring(block, to_z, z):
        whole = put(whole, got, 0, 0, 4 + place)
    return whole.reshape(8, 8, m, n)


def grad_attended_kernel(cot, w, total):
    @pl.when(pl.program_id(0) == 0)
    def _():
        total[...] = jnp.zeros_like(total)

    total[...] += lax.dot_general(
        cot[...], w[0], (((1,), (1,)), ((), ())), preferred_element_type=F32
    )


def grad_attended_part(cot, w):
    rows = cot.shape[0]
    return pl.pallas_call(
        grad_attended_kernel,
        grid=(8,),
        in_specs=[
            pl.BlockSpec((rows, 512), lambda j: (0, j)),
            pl.BlockSpec((1, 512, 512), lambda j: (j, 0, 0)),
        ],
        out_specs=pl.BlockSpec((rows, 512), lambda j: (0, 0)),
        out_shape=jax.ShapeDtypeStruct((rows, 512), F32),
        compiler_params=params(),
        cost_estimate=pl.CostEstimate(
            flops=2 * rows * 4096 * 512, bytes_accessed=rows * 8192 + 4096 * 1024, transcendentals=0
        ),
        name="grad_attended",
    )(cot, w)


def layer_out_kernel(core_ref, att, mine, theirs, video, short):
    n = video.shape[0]
    own = jnp.dot(att[...], mine[0], preferred_element_type=F32).astype(BF)
    other = jnp.dot(att[...], theirs[0], preferred_element_type=F32).astype(BF)
    first = core_ref[0] == 0

    @pl.when(first)
    def _():
        video[:, :512] = own[:n]
        short[:, :512] = own[n:]
        video[:, 512:] = other[:n]
        short[:, 512:] = other[n:]

    @pl.when(jnp.logical_not(first))
    def _():
        video[:, :512] = other[:n]
        short[:, :512] = other[n:]
        video[:, 512:] = own[:n]
        short[:, 512:] = own[n:]


def layer_out(core, att, mine, theirs, nv, ns):
    w = pl.BlockSpec((1, 512, 512), lambda j, s: (j, 0, 0))
    return pl.pallas_call(
        layer_out_kernel,
        grid_spec=pltpu.PrefetchScalarGridSpec(
            num_scalar_prefetch=1,
            grid=(8,),
            in_specs=[pl.BlockSpec((nv + ns, 512), lambda j, s: (0, 0)), w, w],
            out_specs=[
                pl.BlockSpec((nv, 1024), lambda j, s: (0, j)),
                pl.BlockSpec((ns, 1024), lambda j, s: (0, j)),
            ],
        ),
        out_shape=[jax.ShapeDtypeStruct((nv, 8192), BF), jax.ShapeDtypeStruct((ns, 8192), BF)],
        compiler_params=params(),
        cost_estimate=pl.CostEstimate(
            flops=2 * 384 * 8192 * 512, bytes_accessed=16 * 1024 * 1024, transcendentals=0
        ),
        name="layer_out",
    )(core, att, mine, theirs)


TAIL = 16


def term_kernel(tab, *refs, received, bias):
    xa, xb = refs[0:2], refs[2:4]
    ga, gb = refs[4:6]
    got = refs[6 : 6 + received]
    out = refs[-1]
    step = pl.program_id(0)
    n = ga.shape[1]
    dims = (((0,), (0,)), ((), ()))
    left = jnp.concatenate([xa[0][...], xa[1][...]], axis=1)
    total = lax.dot_general(left, ga[...], dims, preferred_element_type=F32)
    left = jnp.concatenate([xb[0][...], xb[1][...]], axis=1)
    total += lax.dot_general(left, gb[...], dims, preferred_element_type=F32)
    for k in range(4):
        where = pl.ds(pl.multiple_of(step * 256 + tab[9 + k] * 64, 64), 64)
        piece = total[k * 64 : (k + 1) * 64]
        for ref in got:
            piece += ref[where, :].astype(F32)
        out[where, :] = piece.astype(BF)

    @pl.when(step == 0)
    def _():
        if bias:
            row = jnp.sum(ga[...].astype(F32), axis=0, keepdims=True)
            row += jnp.sum(gb[...].astype(F32), axis=0, keepdims=True)
            for ref in got:
                row += jnp.sum(ref[1024:, :].astype(F32), axis=0, keepdims=True)
            high = row.astype(BF).astype(F32)
            index = lax.broadcasted_iota(jnp.int32, (TAIL, n), 0)
            out[1024:, :] = jnp.where(
                index == 0, high, jnp.where(index == 1, row - high, 0.0)
            ).astype(BF)
        else:
            out[1024:, :] = jnp.zeros((TAIL, n), BF)


def term_chunk(tab, x_own, x_other, g_own, g_other, got, bias, name):
    rows, n = g_own.shape
    x_spec = lambda k: pl.BlockSpec((rows, 128), lambda j, s: (0, s[2 * j + k]))
    whole = lambda shape: pl.BlockSpec(shape, lambda j, s: (0, 0))
    return pl.pallas_call(
        functools.partial(term_kernel, received=len(got), bias=bias),
        grid_spec=pltpu.PrefetchScalarGridSpec(
            num_scalar_prefetch=1,
            grid=(4,),
            in_specs=[x_spec(0), x_spec(1), x_spec(0), x_spec(1), whole((rows, n)), whole((rows, n))]
            + [whole((1024 + TAIL, n))] * len(got),
            out_specs=whole((1024 + TAIL, n)),
        ),
        out_shape=jax.ShapeDtypeStruct((1024 + TAIL, n), BF),
        compiler_params=params(),
        cost_estimate=pl.CostEstimate(
            flops=2 * 2 * rows * 1024 * n, bytes_accessed=4 * rows * 1024 + 4 * rows * n + 2048 * n,
            transcendentals=0,
        ),
        name=name,
    )(tab, x_own, x_own, x_other, x_other, g_own, g_other, *got)


def tables(at):
    core, z, x = at["c"], at["z"], at["x"]
    y = at["yh"] * 2 + at["yl"]
    result = []
    for far in range(4):
        entries = []
        for step in range(4):
            for yl in range(2):
                zero = (((z + far) % 4) * 2 + yl) * 4 + (x + step) % 4
                one = (((z + step) % 4) * 2 + yl) * 4 + (x + far) % 4
                entries.append(jnp.where(core == 0, zero, one))
        entries.append(jnp.int32(0))
        for yl in range(2):
            for yh in range(2):
                entries.append((yh * 2 + yl - y + 4) % 4)
        result.append(jnp.stack([jnp.asarray(e, jnp.int32) for e in entries]))
    return result


def split_tail(rows):
    high = lax.reduce_precision(rows, 8, 7)
    n = rows.shape[1]
    return jnp.concatenate(
        [high.astype(BF), (rows - high).astype(BF), jnp.zeros((TAIL - 2, n), BF)], axis=0
    )


def fold(parts, chunk, tail):
    total = sum(p[:chunk].astype(F32) for p in parts)
    bias = sum(jnp.sum(p[chunk:].astype(F32), axis=0, keepdims=True) for p in parts) if tail else None
    return total, bias


def scatter(tabs, x_own, x_other, g_own, g_other, bias, name):
    term = lambda far, got: term_chunk(tabs[far], x_own, x_other, g_own, g_other, got, bias, name)
    got = [to_first(term(far, []), far) for far in (2, 1, 3)]
    first = term(0, got)
    tail = [first[1024:]] if bias else []
    chunk = lambda k: jnp.concatenate([first[k * 256 : (k + 1) * 256]] + tail, axis=0)
    got = [to_second(chunk(far), far) for far in (2, 1, 3)]
    total, row = fold([chunk(0)] + got, 256, bias)
    total = total.astype(BF)
    tail = [split_tail(row)] if bias else []
    chunk = lambda k: jnp.concatenate([total[k * 64 : (k + 1) * 64]] + tail, axis=0)
    got = [to_y(chunk(far), far) for far in (2, 1, 3)]
    return fold([chunk(0)] + got, 64, bias)


def rope_angles(positions):
    half_dim = HEAD // 2
    freq_index = jnp.arange(half_dim, dtype=jnp.int32)
    inv_freq = jnp.exp(freq_index.astype(F32) * (-2.0 * THETA_LOG / HEAD))
    first_cut = HEAD // 8
    second_cut = first_cut + 3 * HEAD // 16
    pos_float = positions.astype(F32)
    chosen_pos = jnp.where(
        (freq_index < first_cut)[None, :],
        pos_float[0][:, None],
        jnp.where((freq_index < second_cut)[None, :], pos_float[1][:, None], pos_float[2][:, None]),
    )
    angles = chosen_pos * inv_freq[None, :]
    return (jnp.cos(angles), jnp.sin(angles))


def rotate(tensor, cosines, sine_vals, direction):
    half_dim = HEAD // 2
    wide_cos = cosines[:, None, :]
    wide_sin = sine_vals[:, None, :] * direction
    front_half = tensor[..., :half_dim]
    back_half = tensor[..., half_dim:]
    return jnp.concatenate(
        [
            front_half * wide_cos - back_half * wide_sin,
            back_half * wide_cos + front_half * wide_sin,
        ],
        axis=-1,
    )


def attend(queries, keys_in, values_in, allowed):
    scores = jnp.einsum(
        "rhe,ke->rhk", queries, keys_in, preferred_element_type=F32
    ) * HEAD ** (-0.5)
    scores = jnp.where(allowed, scores, -1e30)
    peak_score = jnp.max(scores, axis=-1, keepdims=True)
    weights = jnp.where(allowed, jnp.exp(scores - peak_score), 0.0)
    weight_sum = jnp.sum(weights, axis=-1, keepdims=True)
    probs = weights / weight_sum
    probs_half = probs.astype(BF)
    attended = jnp.einsum(
        "rhk,ke->rhe", probs_half, values_in, preferred_element_type=F32
    ).astype(BF)
    return (attended, probs, probs_half)


def attend_back(queries, keys_in, values_in, probs, probs_half, grad, delta):
    dprob = jnp.einsum("rhe,ke->rhk", grad, values_in, preferred_element_type=F32)
    dscore = (probs * (dprob - delta[..., None]) * HEAD ** (-0.5)).astype(BF)
    dquery = jnp.einsum("rhk,ke->rhe", dscore, keys_in, preferred_element_type=F32)
    dkey = jnp.einsum("rhk,rhe->ke", dscore, queries, preferred_element_type=F32)
    dvalue = jnp.einsum("rhk,rhe->ke", probs_half, grad, preferred_element_type=F32)
    return dquery, dkey, dvalue


def per_device(
    w_qkv, qkv_bias, w_out, video_x, video_pos, short_x, short_pos, short_seg, video_cot, short_cot
):
    at = {name: lax.axis_index(name) for name in AXES}
    core = at["c"].astype(jnp.int32)[None]
    tabs = tables(at)
    nv, ns = video_x.shape[1], short_x.shape[1]
    rows = nv + ns

    w_half = lax.dynamic_slice(w_qkv, (at["c"] * 512, 0), (512, 768)).reshape(8, 64, 768)
    qkv_whole = gather(w_half[:4], w_half[4:], at).reshape(4096, 768)
    wo_half = weight_half(core, w_out)
    wo = gather(wo_half[:4], wo_half[4:], at)
    wo = wo.transpose(1, 0, 2, 3).reshape(8, 512, 512)
    wo_other = other_core(wo)

    x_own, x_send = column_halves(core, video_x[0], short_x[0])
    x_other = other_core(x_send)
    c_own, c_send = column_halves(core, video_cot[0], short_cot[0])
    c_other = other_core(c_send)

    places = jnp.concatenate([video_pos[:, 0, :], short_pos[:, 0, :]], axis=1)
    cosines, sine_vals = rope_angles(places)

    part = other_core(jnp.dot(x_other, qkv_whole, preferred_element_type=F32))
    projected = (
        jnp.dot(x_own, qkv_whole, preferred_element_type=F32) + part + qkv_bias[None, :]
    )
    key_local = rotate(
        projected[:, ATT : ATT + HEAD].reshape(rows, 1, HEAD), cosines, sine_vals, 1.0
    )[:, 0].astype(BF)
    value_local = projected[:, ATT + HEAD :].astype(BF)
    both_group = lax.all_gather(
        jnp.concatenate([key_local[:nv], value_local[:nv]], axis=1), GRP, axis=0, tiled=True
    )
    keys_group, values_group = both_group[:, :HEAD], both_group[:, HEAD:]
    queries = rotate(
        projected[:, :ATT].reshape(rows, QH, HEAD), cosines, sine_vals, 1.0
    ).astype(BF)

    grad_att_part = other_core(grad_attended_part(c_other, wo))
    grad_attended = (grad_attended_part(c_own, wo) + grad_att_part).astype(BF)

    position = jnp.arange(ns, dtype=jnp.int32)
    segment = short_seg[0]
    short_allowed = (
        (segment[None, :] == segment[:, None]) & (position[None, :] <= position[:, None])
    )[:, None, :]
    short_att, short_probs, short_half = attend(
        queries[nv:], key_local[nv:], value_local[nv:], short_allowed
    )

    first_row = ((at["z"] * 2 + at["yl"]) * 2 + at["c"]) * nv
    key_count = keys_group.shape[0]
    query_at = first_row + jnp.arange(nv, dtype=jnp.int32)
    video_allowed = (jnp.arange(key_count, dtype=jnp.int32)[None, :] <= query_at[:, None])[
        :, None, :
    ]
    video_att, video_probs, video_half = attend(
        queries[:nv], keys_group, values_group, video_allowed
    )
    attended = jnp.concatenate([video_att, short_att], axis=0)
    flat = attended.reshape(rows, ATT)
    flat_other = other_core(flat)

    grad_heads = grad_attended.reshape(rows, QH, HEAD)
    deltas = jnp.sum(grad_heads.astype(F32) * attended.astype(F32), axis=-1)
    video_dq, video_dk, video_dv = attend_back(
        queries[:nv], keys_group, values_group, video_probs, video_half, grad_heads[:nv], deltas[:nv]
    )
    to_owner = jnp.concatenate([video_dk, video_dv], axis=1).astype(BF)
    from_all = lax.all_to_all(to_owner, GRP, 0, 0, tiled=True)
    key_value = jnp.sum(from_all.reshape(16, nv, 2 * HEAD).astype(F32), axis=0)
    short_dq, short_dk, short_dv = attend_back(
        queries[nv:], key_local[nv:], value_local[nv:], short_probs, short_half, grad_heads[nv:], deltas[nv:]
    )

    grad_out, _ = scatter(tabs, c_own, c_other, flat, flat_other, False, "term_out")
    video_y, short_y = layer_out(core, flat, wo, wo_other, nv, ns)

    grad_queries = rotate(
        jnp.concatenate([video_dq, short_dq], axis=0), cosines, sine_vals, -1.0
    ).reshape(rows, ATT).astype(BF)
    grad_q, bias_q = scatter(
        tabs, x_own, x_other, grad_queries, other_core(grad_queries), True, "term_q"
    )
    grad_keys = rotate(
        jnp.concatenate([key_value[:, :HEAD], short_dk], axis=0)[:, None, :], cosines, sine_vals, -1.0
    )[:, 0]
    grad_values = jnp.concatenate([key_value[:, HEAD:], short_dv], axis=0)
    grad_kv_rows = jnp.concatenate([grad_keys, grad_values], axis=1).astype(BF)
    grad_kv, bias_kv = scatter(
        tabs, x_own, x_other, grad_kv_rows, other_core(grad_kv_rows), True, "term_kv"
    )
    return (
        video_y[None],
        short_y[None],
        jnp.concatenate([grad_q, grad_kv], axis=1),
        grad_out.T,
        jnp.concatenate([bias_q, bias_kv], axis=1)[0],
    )


def solution(mesh):
    fine = Mesh(mesh.devices.reshape(SIZES), AXES)
    return jax.shard_map(
        per_device,
        mesh=fine,
        in_specs=(
            P(DP, None),
            P(),
            P(DP, None),
            P(DP, GRP, None),
            P(None, DP, GRP),
            P(DP + GRP, None, None),
            P(None, DP + GRP, None),
            P(DP + GRP, None),
            P(DP, GRP, None),
            P(DP + GRP, None, None),
        ),
        out_specs=(
            P(DP, GRP, None),
            P(DP + GRP, None, None),
            P(GRP + DP, None),
            P(None, GRP + DP),
            P(),
        ),
        check_vma=False,
    )
```

```python
import functools

import jax
import jax.numpy as jnp
from jax import lax
from jax.experimental import pallas as pl
from jax.experimental.pallas import tpu as pltpu
from jax.sharding import Mesh
from jax.sharding import PartitionSpec as P

HEAD = 128
QH = 4
ATT = QH * HEAD
SCALE = HEAD ** (-0.5)
AXES = ("z", "yl", "c", "x", "yh")
SIZES = (4, 2, 2, 4, 2)
GRP = ("z", "yl", "c")
DP = ("x", "yh")
BF = jnp.bfloat16
F32 = jnp.float32
THETA_LOG = 13.815510557964274
STREAM = 52


def device_index(z, y, c, x):
    z, y, c, x = z % 4, y % 4, c % 2, x % 4
    return (((z * 2 + y % 2) * 2 + c) * 4 + x) * 2 + y // 2


def pairs(target):
    result = []
    for z in range(4):
        for y in range(4):
            for c in range(2):
                for x in range(4):
                    result.append((device_index(z, y, c, x), device_index(*target(z, y, c, x))))
    return result


def move(value, target):
    return lax.ppermute(value, AXES, pairs(target))


def other_core(value):
    return move(value, lambda z, y, c, x: (z, y, c + 1, x))


def to_x(value, step):
    return move(value, lambda z, y, c, x: (z, y, c, x + step))


def to_z(value, step):
    return move(value, lambda z, y, c, x: (z + step, y, c, x))


def to_y(value, step):
    return move(value, lambda z, y, c, x: (z, y + step, c, x))


def across(value):
    return move(value, lambda z, y, c, x: (z, 3 - y, c, x))


def to_x_or_across(value, step):
    return move(
        value, lambda z, y, c, x: (z, y, c, x + step) if c == 0 else (z, 3 - y, c, x)
    )


def to_first(value, step):
    return move(
        value, lambda z, y, c, x: (z + step, y, c, x) if c == 0 else (z, y, c, x + step)
    )


def to_second(value, step):
    return move(
        value, lambda z, y, c, x: (z, y, c, x + step) if c == 0 else (z + step, y, c, x)
    )


def call(kernel, name, grid, ins, outs, shapes, tab=None, flops=0, traffic=0, scratch=(), limit=24):
    spec = lambda pair: pl.BlockSpec(*pair)
    single = not isinstance(shapes, list)
    in_specs = [spec(i) for i in ins]
    out_specs = spec(outs[0]) if single else [spec(o) for o in outs]
    cost = pl.CostEstimate(flops=flops, bytes_accessed=traffic, transcendentals=0)
    options = dict(
        out_shape=shapes,
        compiler_params=pltpu.CompilerParams(vmem_limit_bytes=limit * 1024 * 1024),
        cost_estimate=cost,
        name=name,
    )
    if tab is None:
        return pl.pallas_call(
            kernel, grid=grid, in_specs=in_specs, out_specs=out_specs, scratch_shapes=scratch, **options
        )
    grid_spec = pltpu.PrefetchScalarGridSpec(
        num_scalar_prefetch=1, grid=grid, in_specs=in_specs, out_specs=out_specs, scratch_shapes=scratch
    )
    return functools.partial(pl.pallas_call(kernel, grid_spec=grid_spec, **options), tab)


def shaped(shape, kind=BF):
    return jax.ShapeDtypeStruct(shape, kind)


def halves_kernel(core_ref, *refs):
    out = refs[4]
    n = refs[0].shape[0]
    for k in range(2):
        out[:n, k * 512 : (k + 1) * 512] = refs[k][...]
        out[n:, k * 512 : (k + 1) * 512] = refs[2 + k][...]


def halves(core, video, short):
    nv, ns = video.shape[0], short.shape[0]
    theirs = lambda n, k: ((n, 512), lambda j, s: (0, 4 * j + 2 * k + s[0]))
    return call(
        halves_kernel, "halves", (4,), [theirs(nv, 0), theirs(nv, 1), theirs(ns, 0), theirs(ns, 1)],
        [((nv + ns, 1024), lambda j, s: (0, j))], shaped((nv + ns, 4096)), core,
        traffic=4 * (nv + ns) * 4096, limit=STREAM,
    )(video, video, short, short)


def turn_kernel(tab, video, short, other, out):
    nv, rows = video.shape[0], other.shape[0]
    step = pl.program_id(0)
    first, second, third = video[...].T, short[...].T, other[...].T
    for k in range(8):
        where = pl.ds(pl.multiple_of(tab[1 + step * 8 + k] * 64, 64), 64)
        out[where, :nv] = first[k * 64 : (k + 1) * 64]
        out[where, nv:rows] = second[k * 64 : (k + 1) * 64]
        out[where, rows:] = third[k * 64 : (k + 1) * 64]


def turned(tab, video, short, other):
    nv, ns = video.shape[0], short.shape[0]
    rows = nv + ns
    own = lambda n: ((n, 512), lambda j, s: (0, 2 * j + s[0]))
    return call(
        turn_kernel, "turned", (8,),
        [own(nv), own(ns), ((rows, 512), lambda j, s: (0, j))],
        [((4096, 2 * rows), lambda j, s: (0, 0))], shaped((4096, 2 * rows)), tab,
        traffic=8 * rows * 4096, limit=STREAM,
    )(video, short, other)


def weight_quarter_kernel(tab, block, out):
    out[0] = block[...]


def weight_quarter(tab, w):
    return call(
        weight_quarter_kernel, "weight_quarter", (2,),
        [((64, 512), lambda j, s: (0, 2 * (2 * s[1] + j) + s[0]))],
        [((1, 64, 512), lambda j, s: (j, 0, 0))], shaped((2, 64, 512)), tab, traffic=4 * 64 * 1024,
    )(w)


def project_kernel(tab, *refs, parts, added):
    video, short, other = refs[:3]
    weights = refs[3 : 3 + parts]
    out_own, out_other = refs[-2:]
    nv = video.shape[0]
    step = pl.program_id(0)

    for k in range(parts):

        @pl.when(step == k)
        def _(k=k):
            w = weights[k][...]
            first = jnp.dot(video[...], w, preferred_element_type=F32)
            second = jnp.dot(short[...], w, preferred_element_type=F32)
            third = jnp.dot(other[...], w, preferred_element_type=F32)
            if k == 0 and added:
                before_own, before_other = refs[3 + parts : 5 + parts]
                out_own[:nv] = before_own[:nv] + first
                out_own[nv:] = before_own[nv:] + second
                out_other[...] = before_other[...] + third
            elif k == 0:
                out_own[:nv], out_own[nv:], out_other[...] = first, second, third
            else:
                out_own[:nv] += first
                out_own[nv:] += second
                out_other[...] += third


def project(tab, video, short, other, weights, before=()):
    nv, ns, parts = video.shape[0], short.shape[0], len(weights)
    rows = nv + ns
    own = lambda n: ((n, 512), lambda j, s: (0, 2 * s[1 + j] + s[0]))
    whole = lambda shape: (shape, lambda j, s: (0, 0))
    return call(
        functools.partial(project_kernel, parts=parts, added=len(before) > 0), "project", (parts,),
        [own(nv), own(ns), ((rows, 512), lambda j, s: (0, s[1 + j]))]
        + [whole((512, 768))] * parts + [whole((rows, 768))] * len(before),
        [whole((rows, 768))] * 2, [shaped((rows, 768), F32)] * 2, tab,
        flops=4 * rows * 512 * 768 * parts, traffic=parts * (512 * 768 * 2 + rows * 2048) + rows * 768 * 8,
        limit=STREAM,
    )(video, short, other, *weights, *before)


def spin(block, cosines, sines):
    return block * cosines + pltpu.roll(block, HEAD // 2, 1) * sines


def heads_kernel(near, near_got, far, far_got, bias, cosines, sines, queries, keys_values):
    total = near[...] + near_got[...] + far[...] + far_got[...] + bias[...]
    for h in range(QH):
        part = slice(h * HEAD, (h + 1) * HEAD)
        queries[:, part] = spin(total[:, part], cosines[...], sines[...]).astype(BF)
    keys_values[:, :HEAD] = spin(total[:, ATT : ATT + HEAD], cosines[...], sines[...]).astype(BF)
    keys_values[:, HEAD:] = total[:, ATT + HEAD :].astype(BF)


def heads(near, near_got, far, far_got, bias, cosines, sines):
    rows = near.shape[0]
    at = lambda i: (i, 0)
    big, small = ((128, 768), at), ((128, HEAD), at)
    return call(
        heads_kernel, "heads", (rows // 128,),
        [big, big, big, big, ((1, 768), lambda i: (0, 0)), small, small],
        [((128, ATT), at), ((128, 2 * HEAD), at)],
        [shaped((rows, ATT)), shaped((rows, 2 * HEAD))], traffic=rows * 768 * 18,
    )(near, near_got, far, far_got, bias, cosines, sines)


def stacked(block, count):
    return jnp.concatenate([block[:, h * HEAD : (h + 1) * HEAD] for h in range(count)], axis=0)


def attention_core(queries, keys, values, grad, allowed):
    nt = (((1,), (1,)), ((), ()))
    scores = lax.dot_general(queries, keys, nt, preferred_element_type=F32) * SCALE
    scores = jnp.where(allowed, scores, -1e30)
    peak = jnp.max(scores, axis=1, keepdims=True)
    weights = jnp.exp(scores - peak)
    probs = weights * (1.0 / jnp.sum(weights, axis=1, keepdims=True))
    probs_half = probs.astype(BF)
    attended = jnp.dot(probs_half, values, preferred_element_type=F32).astype(BF)
    deltas = jnp.sum(grad.astype(F32) * attended.astype(F32), axis=1, keepdims=True)
    dprob = lax.dot_general(grad, values, nt, preferred_element_type=F32)
    dscore = (probs * (dprob - deltas) * SCALE).astype(BF)
    dquery = jnp.dot(dscore, keys, preferred_element_type=F32)
    dkey = jnp.dot(queries.T, dscore, preferred_element_type=F32)
    dvalue = jnp.dot(grad.T, probs_half, preferred_element_type=F32)
    return attended, dquery, dkey, dvalue


def attention_kernel(tab, queries, keys_values, segments, ga, gb, cosines, sines, result, dkv, total, *, video):
    step = pl.program_id(0)
    n = queries.shape[0]
    m = keys_values.shape[0]
    query_at = lax.broadcasted_iota(jnp.int32, (n, m), 0)
    key_at = lax.broadcasted_iota(jnp.int32, (n, m), 1)
    if video:
        allowed = key_at <= query_at + tab[0]
    else:
        allowed = (segments[1] == segments[0][:, :1]) & (key_at <= query_at)
    allowed = jnp.concatenate([allowed, allowed], axis=0)
    grad = (ga[...] + gb[...]).astype(BF)
    attended, dquery, dkey, dvalue = attention_core(
        stacked(queries[...], 2), keys_values[:, :HEAD], keys_values[:, HEAD:], stacked(grad, 2), allowed
    )
    for h in range(2):
        part = slice(h * HEAD, (h + 1) * HEAD)
        result[0, :, part] = attended[h * n : (h + 1) * n]
        result[1, :, part] = spin(dquery[h * n : (h + 1) * n], cosines[...], -sines[...]).astype(BF)

    @pl.when(step == 0)
    def _():
        total[0] = dkey
        total[1] = dvalue

    @pl.when(step == 1)
    def _():
        dkey_all = (total[0] + dkey).T
        if not video:
            dkey_all = spin(dkey_all, cosines[...], -sines[...])
        dkv[:, :HEAD] = dkey_all.astype(BF)
        dkv[:, HEAD:] = (total[1] + dvalue).T.astype(BF)


def attention(video, first_row, start, count, queries, keys_values, segments, ga, gb, cosines, sines):
    m = keys_values.shape[0] if video else count
    n = count
    row = start
    pair = ((n, 2 * HEAD), lambda i, s: (row, i))
    angle = ((n, HEAD), lambda i, s: (row, 0))
    keys = ((m, 2 * HEAD), lambda i, s: (0 if video else row, 0))
    return call(
        functools.partial(attention_kernel, video=video), "video_attention" if video else "short_attention", (2,),
        [pair, keys, (segments.shape, lambda i, s: (0, 0, 0)), pair, pair, angle, angle],
        [((2, n, 2 * HEAD), lambda i, s: (0, 0, i)), ((m, 2 * HEAD), lambda i, s: (0, 0))],
        [shaped((2, n, ATT)), shaped((m, 2 * HEAD))], first_row,
        flops=2 * 5 * QH * n * m * HEAD, traffic=m * 1024, scratch=[pltpu.VMEM((2, HEAD, m), F32)], limit=48,
    )(queries, keys_values, segments, ga, gb, cosines, sines)


def collect_kernel(parts, cosines, sines, out):
    rows = out.shape[0]
    total = jnp.zeros((rows, 2 * HEAD), F32)
    for k in range(parts.shape[0]):
        total += parts[k].astype(F32)
    out[:, :HEAD] = spin(total[:, :HEAD], cosines[...], -sines[...]).astype(BF)
    out[:, HEAD:] = total[:, HEAD:].astype(BF)


def collect(parts, cosines, sines):
    count, rows = parts.shape[:2]
    zero = lambda i: (0, 0)
    return call(
        collect_kernel, "collect", (1,),
        [((count, rows, 2 * HEAD), lambda i: (0, 0, 0)), ((rows, HEAD), zero), ((rows, HEAD), zero)],
        [((rows, 2 * HEAD), zero)], shaped((rows, 2 * HEAD)), traffic=count * rows * 512,
    )(parts, cosines, sines)


W_BLOCK = ((1, 8, 1, 64, 512), lambda j, *s: (j // 2, 0, j % 2, 0, 0))


def whole_weights(ref):
    return ref[0, :, 0].reshape(ATT, 512)


def grad_attended_kernel(core_ref, video, short, other, w, total_own, total_other):
    nv = video.shape[0]

    @pl.when(pl.program_id(0) == 0)
    def _():
        total_own[...] = jnp.zeros_like(total_own)
        total_other[...] = jnp.zeros_like(total_other)

    block = whole_weights(w).T
    total_other[...] += jnp.dot(other[...], block, preferred_element_type=F32)
    total_own[:nv] += jnp.dot(video[...], block, preferred_element_type=F32)
    total_own[nv:] += jnp.dot(short[...], block, preferred_element_type=F32)


def grad_attended_parts(core, video, short, other, w):
    nv, ns = video.shape[0], short.shape[0]
    rows = nv + ns
    own = lambda n: ((n, 512), lambda j, s: (0, 2 * j + s[0]))
    out = ((rows, ATT), lambda j, s: (0, 0))
    return call(
        grad_attended_kernel, "grad_attended", (8,),
        [own(nv), own(ns), ((rows, 512), lambda j, s: (0, j)), W_BLOCK], [out, out],
        [shaped((rows, ATT), F32)] * 2, core, flops=4 * rows * 4096 * 512,
        traffic=rows * 16384 + 4096 * 1024, limit=STREAM,
    )(video, short, other, w)


def layer_out_kernel(tab, video_att, short_att, mine, theirs, video, short):
    for w, at in ((mine, tab[0]), (theirs, 1 - tab[0])):
        block = whole_weights(w)
        where = pl.ds(pl.multiple_of(at * 512, 512), 512)
        video[:, where] = jnp.dot(video_att[0], block, preferred_element_type=F32).astype(BF)
        short[:, where] = jnp.dot(short_att[0], block, preferred_element_type=F32).astype(BF)


def layer_out(tab, video_att, short_att, mine, theirs):
    nv, ns = video_att.shape[1], short_att.shape[1]
    att = lambda n: ((1, n, ATT), lambda j, s: (0, 0, 0))
    return call(
        layer_out_kernel, "layer_out", (8,), [att(nv), att(ns), W_BLOCK, W_BLOCK],
        [((nv, 1024), lambda j, s: (0, j)), ((ns, 1024), lambda j, s: (0, j))],
        [shaped((nv, 8192)), shaped((ns, 8192))], tab,
        flops=2 * (nv + ns) * 8192 * ATT, traffic=8192 * 1024 + (nv + ns) * 16384, limit=STREAM,
    )(video_att, short_att, mine, theirs)


TAIL = 16


def numbers(*entries):
    return jnp.stack([jnp.asarray(e, jnp.int32) for e in entries])


def turn_table(at):
    core, y = at["c"], at["yh"] * 2 + at["yl"]
    order = []
    for tz in range(4):
        for tyl in range(2):
            for tx in range(4):
                for tyh in range(2):
                    dy = (tyh * 2 + tyl - y + 4) % 4
                    order.append(jnp.where(core == 0, tz * 16 + tx * 4 + dy, tx * 16 + tz * 4 + dy))
    return numbers(core, *order)


def term_kernel(tab, cot, tokens, *refs):
    rights, got, out = refs[:4], refs[4:-1], refs[-1]
    right = jnp.concatenate([r[0] for r in rights], axis=0)

    def write(left):
        total = jnp.dot(left[...], right, preferred_element_type=F32)
        for ref in got:
            total += ref[0].astype(F32)
        out[0] = total.astype(BF)

    pl.when(pl.program_id(0) < 2)(lambda: write(cot))
    pl.when(pl.program_id(0) >= 2)(lambda: write(tokens))


def term(place, cot, tokens, rights, got=()):
    wide = cot.shape[1]
    at = lambda i, s: (i // 2, i % 2, 0)
    block = ((1, 512, ATT), at)
    return call(
        term_kernel, "term", (4,),
        [
            ((512, wide), lambda i, s: (2 * s[0] + jnp.minimum(i, 1), 0)),
            ((512, wide), lambda i, s: (2 * s[0] + jnp.maximum(i - 2, 0), 0)),
        ]
        + [((1, r.shape[1], ATT), lambda i, s: (i // 2, 0, 0)) for r in rights] + [block] * len(got),
        [block], shaped((2, 1024, ATT)), numbers(place % 4),
        flops=4 * wide * 1024 * ATT, traffic=4 * wide * 1024 + 4 * wide * ATT + 4096 * ATT, limit=STREAM,
    )(cot, tokens, *rights, *got)


def summed(own, got):
    return sum((g.astype(F32) for g in got), own).astype(BF)


def scatter(places, cot, tokens, rights):
    got = [to_first(term(places[0] + far, cot, tokens, rights), far) for far in (2, 1, 3)]
    first = [f.reshape(2, 4, 256, ATT) for f in [term(places[0], cot, tokens, rights)] + got]

    def rows(far):
        place = (places[1] + far) % 4
        return sum(lax.dynamic_index_in_dim(f, place, 1, keepdims=False).astype(F32) for f in first)

    got = [to_second(rows(far).astype(BF), far) for far in (2, 1, 3)]
    piece = lambda far: sum(
        (g[:, far * 64 : (far + 1) * 64].astype(F32) for g in got), rows(0)[:, far * 64 : (far + 1) * 64]
    )
    late = [to_y(piece(far).astype(BF), far) for far in (2, 1, 3)]
    return sum((g.astype(F32) for g in late), piece(0))


def tail_of(row):
    high = lax.reduce_precision(row, 8, 7)
    n = row.shape[1]
    return jnp.concatenate(
        [high.astype(BF), (row - high).astype(BF), jnp.zeros((TAIL - 6, n), BF)], axis=0
    )


def tail_sum(tails):
    return sum(t[:3].astype(F32) + t[3:6].astype(F32) for t in tails)


def key_term_kernel(tab, left, ga, gb, tail, out):
    right = jnp.concatenate([ga[...], gb[...]], axis=0)
    rows = left[:, :, 0].reshape(1024, left.shape[4])
    out[0, :1024] = jnp.dot(rows, right, preferred_element_type=F32).astype(BF)
    out[0, 1024:] = tail[...]


def key_term(y, left, ga, gb, tail):
    rows, n = ga.shape
    whole = lambda shape: (shape, lambda i, s: (0, 0))
    return call(
        key_term_kernel, "key_term", (4,),
        [
            ((4, 4, 1, 64, 2 * rows), lambda i, s: (0, 0, ((i % 2) * 2 + i // 2 - s[0] + 4) % 4, 0, 0)),
            whole((rows, n)), whole((rows, n)), whole((TAIL, n)),
        ],
        [((1, 1024 + TAIL, n), lambda i, s: (i, 0, 0))], shaped((4, 1024 + TAIL, n)), numbers(y),
        flops=4 * rows * 4096 * n, traffic=4096 * (4 * rows + 2 * n), limit=STREAM,
    )(left.reshape(4, 4, 4, 64, 2 * rows), ga, gb, tail)


LATE_GROUPS = [
    [device_index(a, y, 0, b) if c == 0 else device_index(b, y, 1, a) for a in range(4) for b in range(4)]
    for c in range(2)
    for y in range(4)
]


def scatter_with_tail(terms):
    first = jnp.sum(terms[:, :1024].astype(F32), axis=0).astype(BF).reshape(16, 64, 256)
    tail = tail_of(tail_sum([terms[k, 1024:] for k in range(4)]))
    parts = jnp.concatenate([first, jnp.broadcast_to(tail[None], (16, TAIL, 256))], axis=1)
    parts = lax.all_to_all(parts, AXES, 0, 0, tiled=True, axis_index_groups=LATE_GROUPS)
    total = jnp.sum(parts.astype(F32), axis=0)
    return total[:64], total[64:67] + total[67:70]


def rope_angles(positions):
    half_dim = HEAD // 2
    freq_index = jnp.arange(half_dim, dtype=jnp.int32)
    inv_freq = jnp.exp(freq_index.astype(F32) * (-2.0 * THETA_LOG / HEAD))
    first_cut = HEAD // 8
    second_cut = first_cut + 3 * HEAD // 16
    pos_float = positions.astype(F32)
    chosen_pos = jnp.where(
        (freq_index < first_cut)[None, :],
        pos_float[0][:, None],
        jnp.where((freq_index < second_cut)[None, :], pos_float[1][:, None], pos_float[2][:, None]),
    )
    angles = chosen_pos * inv_freq[None, :]
    cosines, sines = jnp.cos(angles), jnp.sin(angles)
    return (
        jnp.concatenate([cosines, cosines], axis=1),
        jnp.concatenate([-sines, sines], axis=1),
    )


def to_all(value, axes, count):
    return lax.all_to_all(jnp.broadcast_to(value[None], (count,) + value.shape), axes, 0, 0)


def after(value, *others):
    return lax.optimization_barrier((value,) + others)[0]


def per_device(
    w_qkv, qkv_bias, w_out, video_x, video_pos, short_x, short_pos, short_seg, video_cot, short_cot
):
    at = {name: lax.axis_index(name) for name in AXES}
    core = numbers(at["c"])
    order = turn_table(at)
    nv, ns = video_x.shape[1], short_x.shape[1]
    rows = nv + ns
    video_x, short_x, video_cot, short_cot = video_x[0], short_x[0], video_cot[0], short_cot[0]

    mine = lax.dynamic_slice(w_qkv, (at["c"] * 512, 0), (512, 768))
    x_other = other_core(halves(1 - core, video_x, short_x))
    x_turned = turned(order, video_x, short_x, x_other)
    first, third, facing, quarters, x_turned, x_other, c_send = lax.optimization_barrier((
        to_x(mine, 1), to_x(mine, 3), across(mine),
        to_all(weight_quarter(numbers(at["c"], at["z"]), w_out), DP, 8),
        x_turned, x_other, halves(1 - core, video_cot, short_cot),
    ))
    wo = to_all(quarters, ("z",), 4)
    c_other = other_core(c_send)
    relay = lambda near: jnp.where(at["c"] == 0, facing, near)
    shard = lambda step, yh: ((at["x"] - step + 4) % 4) * 2 + yh
    near, off = at["yh"], 1 - at["yh"]
    part = project(
        numbers(at["c"], shard(0, near), shard(1, near), shard(3, near), shard(0, off)),
        video_x, short_x, x_other, [mine, first, third, facing],
    )
    far_first, far_third, second, c_turned, part = lax.optimization_barrier((
        to_x_or_across(relay(first), 1), to_x_or_across(relay(third), 3), to_x(mine, 2),
        turned(order, video_cot, short_cot, c_other), part,
    ))
    near_own, near_other = project(
        numbers(at["c"], shard(2, near), shard(1, off), shard(3, off)),
        video_x, short_x, x_other, [second, far_first, far_third], part,
    )
    far_second, near_own, near_other = lax.optimization_barrier(
        (to_x_or_across(relay(second), 2), near_own, near_other)
    )

    places = jnp.concatenate([video_pos[:, 0, :], short_pos[:, 0, :]], axis=1)
    cosines, sines = rope_angles(places)
    near_other = other_core(near_other)
    far_own, far_other = project(numbers(at["c"], shard(2, off)), video_x, short_x, x_other, [far_second])
    queries, keys_values = heads(
        near_own, near_other, far_own, other_core(far_other), qkv_bias[None], cosines, sines
    )
    wide = jnp.broadcast_to(keys_values[:nv][None], (16, nv, 2 * HEAD))
    wide, wo = lax.optimization_barrier((wide, wo))
    group = lax.all_to_all(wide, GRP, 0, 0).reshape(16 * nv, 2 * HEAD)

    wo_other = other_core(wo)
    grad_own, grad_other = grad_attended_parts(core, video_cot, short_cot, c_other, wo)
    grad_other = other_core(grad_other)

    segment = short_seg[0]
    segments = jnp.stack([jnp.broadcast_to(segment[:, None], (ns, ns)), jnp.broadcast_to(segment[None, :], (ns, ns))])
    first_row = ((at["z"] * 2 + at["yl"]) * 2 + at["c"]) * nv
    cut = lambda a: a[nv:]
    short_result, short_dkv = attention(
        False, numbers(0), 0, ns, cut(queries), cut(keys_values), segments, cut(grad_own), cut(grad_other),
        cut(cosines), cut(sines),
    )
    group, wo_other = lax.optimization_barrier((group, wo_other))
    video_result, video_dkv = attention(
        True, numbers(first_row), 0, nv, queries, group, jnp.zeros((1, 8, 128), jnp.int32), grad_own, grad_other,
        cosines, sines,
    )
    arrived = lax.all_to_all(video_dkv.reshape(16, nv, 2 * HEAD), GRP, 0, 0, tiled=True)

    results = (video_result, short_result, other_core(video_result), other_core(short_result))
    place = jnp.where(at["c"] == 0, at["z"], at["x"])
    second_place = jnp.where(at["c"] == 0, at["x"], at["z"])
    grad_out, grad_q = scatter((place, second_place), c_turned, x_turned, results)

    video_dkv = collect(arrived, cosines[:nv], sines[:nv])
    dkv = jnp.concatenate([video_dkv, short_dkv], axis=0)
    dkv_other = other_core(dkv)
    sum_q = sum(jnp.sum(r[1].astype(F32), axis=0) for r in results).reshape(2, 256)
    sum_kv = jnp.sum(dkv.astype(F32) + dkv_other.astype(F32), axis=0)[None]
    terms = key_term(at["yh"] * 2 + at["yl"], x_turned, dkv, dkv_other, tail_of(jnp.concatenate([sum_q, sum_kv], axis=0)))
    video_y, short_y = layer_out(core, after(video_result, terms), short_result, wo, wo_other)
    terms, video_y, short_y = lax.optimization_barrier(
        (lax.all_to_all(terms, ("yl", "yh"), 0, 0, tiled=True), video_y, short_y)
    )
    grad_kv, bias = scatter_with_tail(terms)
    return (
        video_y[None],
        short_y[None],
        jnp.concatenate([grad_q, grad_kv], axis=1),
        grad_out.T,
        bias.reshape(768),
    )


def solution(mesh):
    fine = Mesh(mesh.devices.reshape(SIZES), AXES)
    return jax.shard_map(
        per_device,
        mesh=fine,
        in_specs=(
            P(DP, None),
            P(),
            P(DP, None),
            P(DP, GRP, None),
            P(None, DP, GRP),
            P(DP + GRP, None, None),
            P(None, DP + GRP, None),
            P(DP + GRP, None),
            P(DP, GRP, None),
            P(DP + GRP, None, None),
        ),
        out_specs=(
            P(DP, GRP, None),
            P(DP + GRP, None, None),
            P(GRP + DP, None),
            P(None, GRP + DP),
            P(),
        ),
        check_vma=False,
    )
```

```python
import functools

import jax
import jax.numpy as jnp
from jax import lax
from jax.experimental import pallas as pl
from jax.experimental.pallas import tpu as pltpu
from jax.sharding import Mesh
from jax.sharding import PartitionSpec as P

HEAD = 128
QH = 4
ATT = QH * HEAD
SCALE = HEAD ** (-0.5)
AXES = ("z", "yl", "c", "x", "yh")
SIZES = (4, 2, 2, 4, 2)
GRP = ("z", "yl", "c")
DP = ("x", "yh")
BF = jnp.bfloat16
F32 = jnp.float32
THETA_LOG = 13.815510557964274
STREAM = 52


def device_index(z, y, c, x):
    z, y, c, x = z % 4, y % 4, c % 2, x % 4
    return (((z * 2 + y % 2) * 2 + c) * 4 + x) * 2 + y // 2


def pairs(target):
    result = []
    for z in range(4):
        for y in range(4):
            for c in range(2):
                for x in range(4):
                    result.append((device_index(z, y, c, x), device_index(*target(z, y, c, x))))
    return result


def move(value, target):
    return lax.ppermute(value, AXES, pairs(target))


def other_core(value):
    return move(value, lambda z, y, c, x: (z, y, c + 1, x))


def to_x(value, step):
    return move(value, lambda z, y, c, x: (z, y, c, x + step))


def to_z(value, step):
    return move(value, lambda z, y, c, x: (z + step, y, c, x))


def to_y(value, step):
    return move(value, lambda z, y, c, x: (z, y + step, c, x))


def across(value):
    return move(value, lambda z, y, c, x: (z, 3 - y, c, x))


def to_x_or_across(value, step):
    return move(
        value, lambda z, y, c, x: (z, y, c, x + step) if c == 0 else (z, 3 - y, c, x)
    )


def to_first(value, step):
    return move(
        value, lambda z, y, c, x: (z + step, y, c, x) if c == 0 else (z, y, c, x + step)
    )


def to_second(value, step):
    return move(
        value, lambda z, y, c, x: (z, y, c, x + step) if c == 0 else (z + step, y, c, x)
    )


def call(kernel, name, grid, ins, outs, shapes, tab=None, flops=0, traffic=0, scratch=(), limit=24):
    spec = lambda pair: pl.BlockSpec(*pair)
    single = not isinstance(shapes, list)
    in_specs = [spec(i) for i in ins]
    out_specs = spec(outs[0]) if single else [spec(o) for o in outs]
    cost = pl.CostEstimate(flops=flops, bytes_accessed=traffic, transcendentals=0)
    options = dict(
        out_shape=shapes,
        compiler_params=pltpu.CompilerParams(vmem_limit_bytes=limit * 1024 * 1024),
        cost_estimate=cost,
        name=name,
    )
    if tab is None:
        return pl.pallas_call(
            kernel, grid=grid, in_specs=in_specs, out_specs=out_specs, scratch_shapes=scratch, **options
        )
    grid_spec = pltpu.PrefetchScalarGridSpec(
        num_scalar_prefetch=1, grid=grid, in_specs=in_specs, out_specs=out_specs, scratch_shapes=scratch
    )
    return functools.partial(pl.pallas_call(kernel, grid_spec=grid_spec, **options), tab)


def shaped(shape, kind=BF):
    return jax.ShapeDtypeStruct(shape, kind)


def halves_kernel(core_ref, *refs):
    out = refs[4]
    n = refs[0].shape[0]
    for k in range(2):
        out[:n, k * 512 : (k + 1) * 512] = refs[k][...]
        out[n:, k * 512 : (k + 1) * 512] = refs[2 + k][...]


def halves(core, video, short):
    nv, ns = video.shape[0], short.shape[0]
    theirs = lambda n, k: ((n, 512), lambda j, s: (0, 4 * j + 2 * k + s[0]))
    return call(
        halves_kernel, "halves", (4,), [theirs(nv, 0), theirs(nv, 1), theirs(ns, 0), theirs(ns, 1)],
        [((nv + ns, 1024), lambda j, s: (0, j))], shaped((nv + ns, 4096)), core,
        traffic=4 * (nv + ns) * 4096, limit=STREAM,
    )(video, video, short, short)


def turn_kernel(tab, video, short, other, out):
    nv, rows = video.shape[0], other.shape[0]
    step = pl.program_id(0)
    first, second, third = video[...].T, short[...].T, other[...].T
    for k in range(8):
        where = pl.ds(pl.multiple_of(tab[1 + step * 8 + k] * 64, 64), 64)
        out[where, :nv] = first[k * 64 : (k + 1) * 64]
        out[where, nv:rows] = second[k * 64 : (k + 1) * 64]
        out[where, rows:] = third[k * 64 : (k + 1) * 64]


def turned(tab, video, short, other):
    nv, ns = video.shape[0], short.shape[0]
    rows = nv + ns
    own = lambda n: ((n, 512), lambda j, s: (0, 2 * j + s[0]))
    return call(
        turn_kernel, "turned", (8,),
        [own(nv), own(ns), ((rows, 512), lambda j, s: (0, j))],
        [((4096, 2 * rows), lambda j, s: (0, 0))], shaped((4096, 2 * rows)), tab,
        traffic=8 * rows * 4096, limit=STREAM,
    )(video, short, other)


def weight_quarter_kernel(tab, block, out):
    out[0] = block[...]


def weight_quarter(tab, w):
    return call(
        weight_quarter_kernel, "weight_quarter", (2,),
        [((64, 512), lambda j, s: (0, 2 * (2 * s[1] + j) + s[0]))],
        [((1, 64, 512), lambda j, s: (j, 0, 0))], shaped((2, 64, 512)), tab, traffic=4 * 64 * 1024,
    )(w)


def project_kernel(tab, *refs, parts, added):
    video, short, other = refs[:3]
    weights = refs[3 : 3 + parts]
    out_own, out_other = refs[-2:]
    nv = video.shape[0]
    step = pl.program_id(0)

    for k in range(parts):

        @pl.when(step == k)
        def _(k=k):
            w = weights[k][...]
            first = jnp.dot(video[...], w, preferred_element_type=F32)
            second = jnp.dot(short[...], w, preferred_element_type=F32)
            third = jnp.dot(other[...], w, preferred_element_type=F32)
            if k == 0 and added:
                before_own, before_other = refs[3 + parts : 5 + parts]
                out_own[:nv] = before_own[:nv] + first
                out_own[nv:] = before_own[nv:] + second
                out_other[...] = before_other[...] + third
            elif k == 0:
                out_own[:nv], out_own[nv:], out_other[...] = first, second, third
            else:
                out_own[:nv] += first
                out_own[nv:] += second
                out_other[...] += third


def project(tab, video, short, other, weights, before=()):
    nv, ns, parts = video.shape[0], short.shape[0], len(weights)
    rows = nv + ns
    own = lambda n: ((n, 512), lambda j, s: (0, 2 * s[1 + j] + s[0]))
    whole = lambda shape: (shape, lambda j, s: (0, 0))
    return call(
        functools.partial(project_kernel, parts=parts, added=len(before) > 0), "project", (parts,),
        [own(nv), own(ns), ((rows, 512), lambda j, s: (0, s[1 + j]))]
        + [whole((512, 768))] * parts + [whole((rows, 768))] * len(before),
        [whole((rows, 768))] * 2, [shaped((rows, 768), F32)] * 2, tab,
        flops=4 * rows * 512 * 768 * parts, traffic=parts * (512 * 768 * 2 + rows * 2048) + rows * 768 * 8,
        limit=STREAM,
    )(video, short, other, *weights, *before)


def spin(block, cosines, sines):
    return block * cosines + pltpu.roll(block, HEAD // 2, 1) * sines


def heads_kernel(near, near_got, far, far_got, bias, cosines, sines, queries, keys_values):
    total = near[...] + near_got[...] + far[...] + far_got[...] + bias[...]
    for h in range(QH):
        part = slice(h * HEAD, (h + 1) * HEAD)
        queries[:, part] = spin(total[:, part], cosines[...], sines[...]).astype(BF)
    keys_values[:, :HEAD] = spin(total[:, ATT : ATT + HEAD], cosines[...], sines[...]).astype(BF)
    keys_values[:, HEAD:] = total[:, ATT + HEAD :].astype(BF)


def heads(near, near_got, far, far_got, bias, cosines, sines):
    rows = near.shape[0]
    at = lambda i: (i, 0)
    big, small = ((128, 768), at), ((128, HEAD), at)
    return call(
        heads_kernel, "heads", (rows // 128,),
        [big, big, big, big, ((1, 768), lambda i: (0, 0)), small, small],
        [((128, ATT), at), ((128, 2 * HEAD), at)],
        [shaped((rows, ATT)), shaped((rows, 2 * HEAD))], traffic=rows * 768 * 18,
    )(near, near_got, far, far_got, bias, cosines, sines)


def stacked(block, count):
    return jnp.concatenate([block[:, h * HEAD : (h + 1) * HEAD] for h in range(count)], axis=0)


def attention_core(queries, keys, values, grad, allowed):
    nt = (((1,), (1,)), ((), ()))
    scores = lax.dot_general(queries, keys, nt, preferred_element_type=F32) * SCALE
    scores = jnp.where(allowed, scores, -1e30)
    peak = jnp.max(scores, axis=1, keepdims=True)
    weights = jnp.exp(scores - peak)
    probs = weights * (1.0 / jnp.sum(weights, axis=1, keepdims=True))
    probs_half = probs.astype(BF)
    attended = jnp.dot(probs_half, values, preferred_element_type=F32).astype(BF)
    deltas = jnp.sum(grad.astype(F32) * attended.astype(F32), axis=1, keepdims=True)
    dprob = lax.dot_general(grad, values, nt, preferred_element_type=F32)
    dscore = (probs * (dprob - deltas) * SCALE).astype(BF)
    dquery = jnp.dot(dscore, keys, preferred_element_type=F32)
    dkey = jnp.dot(queries.T, dscore, preferred_element_type=F32)
    dvalue = jnp.dot(grad.T, probs_half, preferred_element_type=F32)
    return attended, dquery, dkey, dvalue


def attention_kernel(tab, queries, keys_values, segments, ga, gb, cosines, sines, result, dkv, total, *, video):
    step = pl.program_id(0)
    n = queries.shape[0]
    m = keys_values.shape[0]
    query_at = lax.broadcasted_iota(jnp.int32, (n, m), 0)
    key_at = lax.broadcasted_iota(jnp.int32, (n, m), 1)
    if video:
        allowed = key_at <= query_at + tab[0]
    else:
        allowed = (segments[1] == segments[0][:, :1]) & (key_at <= query_at)
    allowed = jnp.concatenate([allowed, allowed], axis=0)
    grad = (ga[...] + gb[...]).astype(BF)
    attended, dquery, dkey, dvalue = attention_core(
        stacked(queries[...], 2), keys_values[:, :HEAD], keys_values[:, HEAD:], stacked(grad, 2), allowed
    )
    for h in range(2):
        part = slice(h * HEAD, (h + 1) * HEAD)
        result[0, :, part] = attended[h * n : (h + 1) * n]
        result[1, :, part] = spin(dquery[h * n : (h + 1) * n], cosines[...], -sines[...]).astype(BF)

    @pl.when(step == 0)
    def _():
        total[0] = dkey
        total[1] = dvalue

    @pl.when(step == 1)
    def _():
        dkey_all = (total[0] + dkey).T
        if not video:
            dkey_all = spin(dkey_all, cosines[...], -sines[...])
        dkv[:, :HEAD] = dkey_all.astype(BF)
        dkv[:, HEAD:] = (total[1] + dvalue).T.astype(BF)


def attention(video, first_row, start, count, queries, keys_values, segments, ga, gb, cosines, sines):
    m = keys_values.shape[0] if video else count
    n = count
    row = start
    pair = ((n, 2 * HEAD), lambda i, s: (row, i))
    angle = ((n, HEAD), lambda i, s: (row, 0))
    keys = ((m, 2 * HEAD), lambda i, s: (0 if video else row, 0))
    return call(
        functools.partial(attention_kernel, video=video), "video_attention" if video else "short_attention", (2,),
        [pair, keys, (segments.shape, lambda i, s: (0, 0, 0)), pair, pair, angle, angle],
        [((2, n, 2 * HEAD), lambda i, s: (0, 0, i)), ((m, 2 * HEAD), lambda i, s: (0, 0))],
        [shaped((2, n, ATT)), shaped((m, 2 * HEAD))], first_row,
        flops=2 * 5 * QH * n * m * HEAD, traffic=m * 1024, scratch=[pltpu.VMEM((2, HEAD, m), F32)], limit=48,
    )(queries, keys_values, segments, ga, gb, cosines, sines)


def collect_kernel(parts, cosines, sines, out):
    rows = out.shape[0]
    total = jnp.zeros((rows, 2 * HEAD), F32)
    for k in range(parts.shape[0]):
        total += parts[k].astype(F32)
    out[:, :HEAD] = spin(total[:, :HEAD], cosines[...], -sines[...]).astype(BF)
    out[:, HEAD:] = total[:, HEAD:].astype(BF)


def collect(parts, cosines, sines):
    count, rows = parts.shape[:2]
    zero = lambda i: (0, 0)
    return call(
        collect_kernel, "collect", (1,),
        [((count, rows, 2 * HEAD), lambda i: (0, 0, 0)), ((rows, HEAD), zero), ((rows, HEAD), zero)],
        [((rows, 2 * HEAD), zero)], shaped((rows, 2 * HEAD)), traffic=count * rows * 512,
    )(parts, cosines, sines)


W_BLOCK = ((1, 8, 1, 64, 512), lambda j, *s: (j // 2, 0, j % 2, 0, 0))


def whole_weights(ref):
    return ref[0, :, 0].reshape(ATT, 512)


def grad_attended_kernel(core_ref, video, short, other, w, total_own, total_other):
    nv = video.shape[0]

    @pl.when(pl.program_id(0) == 0)
    def _():
        total_own[...] = jnp.zeros_like(total_own)
        total_other[...] = jnp.zeros_like(total_other)

    block = whole_weights(w).T
    total_other[...] += jnp.dot(other[...], block, preferred_element_type=F32)
    total_own[:nv] += jnp.dot(video[...], block, preferred_element_type=F32)
    total_own[nv:] += jnp.dot(short[...], block, preferred_element_type=F32)


def grad_attended_parts(core, video, short, other, w):
    nv, ns = video.shape[0], short.shape[0]
    rows = nv + ns
    own = lambda n: ((n, 512), lambda j, s: (0, 2 * j + s[0]))
    out = ((rows, ATT), lambda j, s: (0, 0))
    return call(
        grad_attended_kernel, "grad_attended", (8,),
        [own(nv), own(ns), ((rows, 512), lambda j, s: (0, j)), W_BLOCK], [out, out],
        [shaped((rows, ATT), F32)] * 2, core, flops=4 * rows * 4096 * 512,
        traffic=rows * 16384 + 4096 * 1024, limit=STREAM,
    )(video, short, other, w)


def layer_out_kernel(tab, video_att, short_att, mine, theirs, video, short):
    for w, at in ((mine, tab[0]), (theirs, 1 - tab[0])):
        block = whole_weights(w)
        where = pl.ds(pl.multiple_of(at * 512, 512), 512)
        video[:, where] = jnp.dot(video_att[0], block, preferred_element_type=F32).astype(BF)
        short[:, where] = jnp.dot(short_att[0], block, preferred_element_type=F32).astype(BF)


def layer_out(tab, video_att, short_att, mine, theirs):
    nv, ns = video_att.shape[1], short_att.shape[1]
    att = lambda n: ((1, n, ATT), lambda j, s: (0, 0, 0))
    return call(
        layer_out_kernel, "layer_out", (8,), [att(nv), att(ns), W_BLOCK, W_BLOCK],
        [((nv, 1024), lambda j, s: (0, j)), ((ns, 1024), lambda j, s: (0, j))],
        [shaped((nv, 8192)), shaped((ns, 8192))], tab,
        flops=2 * (nv + ns) * 8192 * ATT, traffic=8192 * 1024 + (nv + ns) * 16384, limit=STREAM,
    )(video_att, short_att, mine, theirs)


TAIL = 16


def numbers(*entries):
    return jnp.stack([jnp.asarray(e, jnp.int32) for e in entries])


def turn_table(at):
    core, y = at["c"], at["yh"] * 2 + at["yl"]
    order = []
    for tz in range(4):
        for tyl in range(2):
            for tx in range(4):
                for tyh in range(2):
                    dy = (tyh * 2 + tyl - y + 4) % 4
                    order.append(jnp.where(core == 0, tz * 16 + tx * 4 + dy, tx * 16 + tz * 4 + dy))
    return numbers(core, *order)


def term_kernel(tab, cot, tokens, *refs):
    rights, got, out = refs[:4], refs[4:-1], refs[-1]
    right = jnp.concatenate([r[0] for r in rights], axis=0)

    def write(left):
        total = jnp.dot(left[...], right, preferred_element_type=F32)
        for ref in got:
            total += ref[0].astype(F32)
        out[0] = total.astype(BF)

    pl.when(pl.program_id(0) < 2)(lambda: write(cot))
    pl.when(pl.program_id(0) >= 2)(lambda: write(tokens))


def term(place, cot, tokens, rights, got=()):
    wide = cot.shape[1]
    at = lambda i, s: (i // 2, i % 2, 0)
    block = ((1, 512, ATT), at)
    return call(
        term_kernel, "term", (4,),
        [
            ((512, wide), lambda i, s: (2 * s[0] + jnp.minimum(i, 1), 0)),
            ((512, wide), lambda i, s: (2 * s[0] + jnp.maximum(i - 2, 0), 0)),
        ]
        + [((1, r.shape[1], ATT), lambda i, s: (i // 2, 0, 0)) for r in rights] + [block] * len(got),
        [block], shaped((2, 1024, ATT)), numbers(place % 4),
        flops=4 * wide * 1024 * ATT, traffic=4 * wide * 1024 + 4 * wide * ATT + 4096 * ATT, limit=STREAM,
    )(cot, tokens, *rights, *got)


def summed(own, got):
    return sum((g.astype(F32) for g in got), own).astype(BF)


def scatter(places, cot, tokens, rights, parts):
    got = [to_first(term(places[0] + far, cot, tokens, rights), far) for far in (2, 1, 3)]
    first = [f.reshape(2, 4, 256, ATT) for f in [term(places[0], cot, tokens, rights)] + got]

    def rows(far):
        place = (places[1] + far) % 4
        return sum(lax.dynamic_index_in_dim(f, place, 1, keepdims=False).astype(F32) for f in first)

    got = []
    for far in (2, 1, 3):
        chunk = rows(far).astype(BF)
        *first, chunk = lax.optimization_barrier((*first, chunk))
        got.append(to_second(chunk, far))
    *got, parts = lax.optimization_barrier((*got, parts))
    piece = lambda far: sum(
        (g[:, far * 64 : (far + 1) * 64].astype(F32) for g in got), rows(0)[:, far * 64 : (far + 1) * 64]
    )
    late = [to_y(piece(far).astype(BF), far) for far in (2, 1, 3)]
    return sum((g.astype(F32) for g in late), piece(0)), parts


def tail_of(row):
    high = lax.reduce_precision(row, 8, 7)
    n = row.shape[1]
    return jnp.concatenate(
        [high.astype(BF), (row - high).astype(BF), jnp.zeros((TAIL - 6, n), BF)], axis=0
    )


def tail_sum(tails):
    return sum(t[:3].astype(F32) + t[3:6].astype(F32) for t in tails)


def key_term_kernel(tab, left, ga, gb, tail, out):
    right = jnp.concatenate([ga[...], gb[...]], axis=0)
    rows = left[:, :, 0].reshape(1024, left.shape[4])
    out[0, :1024] = jnp.dot(rows, right, preferred_element_type=F32).astype(BF)
    out[0, 1024:] = tail[...]


def key_term(y, left, ga, gb, tail):
    rows, n = ga.shape
    whole = lambda shape: (shape, lambda i, s: (0, 0))
    return call(
        key_term_kernel, "key_term", (4,),
        [
            ((4, 4, 1, 64, 2 * rows), lambda i, s: (0, 0, ((i % 2) * 2 + i // 2 - s[0] + 4) % 4, 0, 0)),
            whole((rows, n)), whole((rows, n)), whole((TAIL, n)),
        ],
        [((1, 1024 + TAIL, n), lambda i, s: (i, 0, 0))], shaped((4, 1024 + TAIL, n)), numbers(y),
        flops=4 * rows * 4096 * n, traffic=4096 * (4 * rows + 2 * n), limit=STREAM,
    )(left.reshape(4, 4, 4, 64, 2 * rows), ga, gb, tail)


LATE_GROUPS = [
    [device_index(a, y, 0, b) if c == 0 else device_index(b, y, 1, a) for a in range(4) for b in range(4)]
    for c in range(2)
    for y in range(4)
]


def key_parts(terms):
    first = jnp.sum(terms[:, :1024].astype(F32), axis=0).astype(BF).reshape(16, 64, 256)
    tail = tail_of(tail_sum([terms[k, 1024:] for k in range(4)]))
    return jnp.concatenate([first, jnp.broadcast_to(tail[None], (16, TAIL, 256))], axis=1)


def key_sum(parts):
    parts = lax.all_to_all(parts, AXES, 0, 0, tiled=True, axis_index_groups=LATE_GROUPS)
    total = jnp.sum(parts.astype(F32), axis=0)
    return total[:64], total[64:67] + total[67:70]


def rope_angles(positions):
    half_dim = HEAD // 2
    freq_index = jnp.arange(half_dim, dtype=jnp.int32)
    inv_freq = jnp.exp(freq_index.astype(F32) * (-2.0 * THETA_LOG / HEAD))
    first_cut = HEAD // 8
    second_cut = first_cut + 3 * HEAD // 16
    pos_float = positions.astype(F32)
    chosen_pos = jnp.where(
        (freq_index < first_cut)[None, :],
        pos_float[0][:, None],
        jnp.where((freq_index < second_cut)[None, :], pos_float[1][:, None], pos_float[2][:, None]),
    )
    angles = chosen_pos * inv_freq[None, :]
    cosines, sines = jnp.cos(angles), jnp.sin(angles)
    return (
        jnp.concatenate([cosines, cosines], axis=1),
        jnp.concatenate([-sines, sines], axis=1),
    )


def to_all(value, axes, count):
    return lax.all_to_all(jnp.broadcast_to(value[None], (count,) + value.shape), axes, 0, 0)


def after(value, *others):
    return lax.optimization_barrier((value,) + others)[0]


def per_device(
    w_qkv, qkv_bias, w_out, video_x, video_pos, short_x, short_pos, short_seg, video_cot, short_cot
):
    at = {name: lax.axis_index(name) for name in AXES}
    core = numbers(at["c"])
    order = turn_table(at)
    nv, ns = video_x.shape[1], short_x.shape[1]
    rows = nv + ns
    video_x, short_x, video_cot, short_cot = video_x[0], short_x[0], video_cot[0], short_cot[0]

    mine = lax.dynamic_slice(w_qkv, (at["c"] * 512, 0), (512, 768))
    x_other = other_core(halves(1 - core, video_x, short_x))
    x_turned = turned(order, video_x, short_x, x_other)
    quarters = to_all(weight_quarter(numbers(at["c"], at["z"]), w_out), DP, 8)
    wide, later_cot, x_turned = lax.optimization_barrier(
        (jnp.broadcast_to(quarters[None], (4,) + quarters.shape), video_cot, x_turned)
    )
    wo = lax.all_to_all(wide, ("z",), 0, 0)
    first, third, facing, x_turned, x_other, c_send = lax.optimization_barrier((
        to_x(mine, 1), to_x(mine, 3), across(mine), x_turned, x_other,
        halves(1 - core, later_cot, short_cot),
    ))
    c_other = other_core(c_send)
    relay = lambda near: jnp.where(at["c"] == 0, facing, near)
    shard = lambda step, yh: ((at["x"] - step + 4) % 4) * 2 + yh
    near, off = at["yh"], 1 - at["yh"]
    part = project(
        numbers(at["c"], shard(0, near), shard(1, near), shard(3, near), shard(0, off)),
        video_x, short_x, x_other, [mine, first, third, facing],
    )
    far_first, far_third, second, c_turned, part = lax.optimization_barrier((
        to_x_or_across(relay(first), 1), to_x_or_across(relay(third), 3), to_x(mine, 2),
        turned(order, video_cot, short_cot, c_other), part,
    ))
    near_own, near_other = project(
        numbers(at["c"], shard(2, near), shard(1, off), shard(3, off)),
        video_x, short_x, x_other, [second, far_first, far_third], part,
    )
    far_second, near_own, near_other = lax.optimization_barrier(
        (to_x_or_across(relay(second), 2), near_own, near_other)
    )

    places = jnp.concatenate([video_pos[:, 0, :], short_pos[:, 0, :]], axis=1)
    cosines, sines = rope_angles(places)
    near_other = other_core(near_other)
    far_own, far_other = project(numbers(at["c"], shard(2, off)), video_x, short_x, x_other, [far_second])
    queries, keys_values = heads(
        near_own, near_other, far_own, other_core(far_other), qkv_bias[None], cosines, sines
    )
    wide = jnp.broadcast_to(keys_values[:nv][None], (16, nv, 2 * HEAD))
    wide, wo = lax.optimization_barrier((wide, wo))
    group = lax.all_to_all(wide, GRP, 0, 0).reshape(16 * nv, 2 * HEAD)

    wo_other = other_core(wo)
    grad_own, grad_other = grad_attended_parts(core, video_cot, short_cot, c_other, wo)
    grad_other = other_core(grad_other)

    segment = short_seg[0]
    segments = jnp.stack([jnp.broadcast_to(segment[:, None], (ns, ns)), jnp.broadcast_to(segment[None, :], (ns, ns))])
    first_row = ((at["z"] * 2 + at["yl"]) * 2 + at["c"]) * nv
    cut = lambda a: a[nv:]
    short_result, short_dkv = attention(
        False, numbers(0), 0, ns, cut(queries), cut(keys_values), segments, cut(grad_own), cut(grad_other),
        cut(cosines), cut(sines),
    )
    group, wo_other = lax.optimization_barrier((group, wo_other))
    video_result, video_dkv = attention(
        True, numbers(first_row), 0, nv, queries, group, jnp.zeros((1, 8, 128), jnp.int32), grad_own, grad_other,
        cosines, sines,
    )
    arrived = lax.all_to_all(video_dkv.reshape(16, nv, 2 * HEAD), GRP, 0, 0, tiled=True)

    results = (video_result, short_result, other_core(video_result), other_core(short_result))
    place = jnp.where(at["c"] == 0, at["z"], at["x"])
    second_place = jnp.where(at["c"] == 0, at["x"], at["z"])

    video_dkv = collect(arrived, cosines[:nv], sines[:nv])
    dkv = jnp.concatenate([video_dkv, short_dkv], axis=0)
    dkv_other = other_core(dkv)
    sum_q = sum(jnp.sum(r[1].astype(F32), axis=0) for r in results).reshape(2, 256)
    sum_kv = jnp.sum(dkv.astype(F32) + dkv_other.astype(F32), axis=0)[None]
    terms = key_term(at["yh"] * 2 + at["yl"], x_turned, dkv, dkv_other, tail_of(jnp.concatenate([sum_q, sum_kv], axis=0)))
    video_y, short_y = layer_out(core, after(video_result, terms), short_result, wo, wo_other)
    terms, video_y, short_y = lax.optimization_barrier(
        (lax.all_to_all(terms, ("yl", "yh"), 0, 0, tiled=True), video_y, short_y)
    )
    (grad_out, grad_q), parts = scatter(
        (place, second_place), c_turned, x_turned, results, key_parts(terms)
    )
    grad_kv, bias = key_sum(parts)
    return (
        video_y[None],
        short_y[None],
        jnp.concatenate([grad_q, grad_kv], axis=1),
        grad_out.T,
        bias.reshape(768),
    )


def solution(mesh):
    fine = Mesh(mesh.devices.reshape(SIZES), AXES)
    return jax.shard_map(
        per_device,
        mesh=fine,
        in_specs=(
            P(DP, None),
            P(),
            P(DP, None),
            P(DP, GRP, None),
            P(None, DP, GRP),
            P(DP + GRP, None, None),
            P(None, DP + GRP, None),
            P(DP + GRP, None),
            P(DP, GRP, None),
            P(DP + GRP, None, None),
        ),
        out_specs=(
            P(DP, GRP, None),
            P(DP + GRP, None, None),
            P(GRP + DP, None),
            P(None, GRP + DP),
            P(),
        ),
        check_vma=False,
    )
```

```python
import functools

import jax
import jax.numpy as jnp
from jax import lax
from jax.experimental import pallas as pl
from jax.experimental.pallas import tpu as pltpu
from jax.sharding import Mesh
from jax.sharding import PartitionSpec as P

HEAD = 128
QH = 4
ATT = QH * HEAD
SCALE = HEAD ** (-0.5)
AXES = ("z", "yl", "c", "x", "yh")
SIZES = (4, 2, 2, 4, 2)
GRP = ("z", "yl", "c")
DP = ("x", "yh")
BF = jnp.bfloat16
F32 = jnp.float32
THETA_LOG = 13.815510557964274
STREAM = 52


def device_index(z, y, c, x):
    z, y, c, x = z % 4, y % 4, c % 2, x % 4
    return (((z * 2 + y % 2) * 2 + c) * 4 + x) * 2 + y // 2


def pairs(target):
    result = []
    for z in range(4):
        for y in range(4):
            for c in range(2):
                for x in range(4):
                    result.append((device_index(z, y, c, x), device_index(*target(z, y, c, x))))
    return result


def move(value, target):
    return lax.ppermute(value, AXES, pairs(target))


def other_core(value):
    return move(value, lambda z, y, c, x: (z, y, c + 1, x))


def to_x(value, step):
    return move(value, lambda z, y, c, x: (z, y, c, x + step))


def to_z(value, step):
    return move(value, lambda z, y, c, x: (z + step, y, c, x))


def to_y(value, step):
    return move(value, lambda z, y, c, x: (z, y + step, c, x))


def across(value):
    return move(value, lambda z, y, c, x: (z, 3 - y, c, x))


def to_x_or_across(value, step):
    return move(
        value, lambda z, y, c, x: (z, y, c, x + step) if c == 0 else (z, 3 - y, c, x)
    )


def to_first(value, step):
    return move(
        value, lambda z, y, c, x: (z + step, y, c, x) if c == 0 else (z, y, c, x + step)
    )


def to_second(value, step):
    return move(
        value, lambda z, y, c, x: (z, y, c, x + step) if c == 0 else (z + step, y, c, x)
    )


def call(kernel, name, grid, ins, outs, shapes, tab=None, flops=0, traffic=0, scratch=(), limit=24):
    spec = lambda pair: pl.BlockSpec(*pair)
    single = not isinstance(shapes, list)
    in_specs = [spec(i) for i in ins]
    out_specs = spec(outs[0]) if single else [spec(o) for o in outs]
    cost = pl.CostEstimate(flops=flops, bytes_accessed=traffic, transcendentals=0)
    options = dict(
        out_shape=shapes,
        compiler_params=pltpu.CompilerParams(vmem_limit_bytes=limit * 1024 * 1024),
        cost_estimate=cost,
        name=name,
    )
    if tab is None:
        return pl.pallas_call(
            kernel, grid=grid, in_specs=in_specs, out_specs=out_specs, scratch_shapes=scratch, **options
        )
    grid_spec = pltpu.PrefetchScalarGridSpec(
        num_scalar_prefetch=1, grid=grid, in_specs=in_specs, out_specs=out_specs, scratch_shapes=scratch
    )
    return functools.partial(pl.pallas_call(kernel, grid_spec=grid_spec, **options), tab)


def shaped(shape, kind=BF):
    return jax.ShapeDtypeStruct(shape, kind)


def halves_kernel(core_ref, *refs):
    out = refs[4]
    n = refs[0].shape[0]
    for k in range(2):
        out[:n, k * 512 : (k + 1) * 512] = refs[k][...]
        out[n:, k * 512 : (k + 1) * 512] = refs[2 + k][...]


def halves(core, video, short):
    nv, ns = video.shape[0], short.shape[0]
    theirs = lambda n, k: ((n, 512), lambda j, s: (0, 4 * j + 2 * k + s[0]))
    return call(
        halves_kernel, "halves", (4,), [theirs(nv, 0), theirs(nv, 1), theirs(ns, 0), theirs(ns, 1)],
        [((nv + ns, 1024), lambda j, s: (0, j))], shaped((nv + ns, 4096)), core,
        traffic=4 * (nv + ns) * 4096, limit=STREAM,
    )(video, video, short, short)


def turn_kernel(tab, video, short, other, out):
    nv, rows = video.shape[0], other.shape[0]
    step = pl.program_id(0)
    first, second, third = video[...].T, short[...].T, other[...].T
    for k in range(8):
        where = pl.ds(pl.multiple_of(tab[1 + step * 8 + k] * 64, 64), 64)
        out[where, :nv] = first[k * 64 : (k + 1) * 64]
        out[where, nv:rows] = second[k * 64 : (k + 1) * 64]
        out[where, rows:] = third[k * 64 : (k + 1) * 64]


def turned(tab, video, short, other):
    nv, ns = video.shape[0], short.shape[0]
    rows = nv + ns
    own = lambda n: ((n, 512), lambda j, s: (0, 2 * j + s[0]))
    return call(
        turn_kernel, "turned", (8,),
        [own(nv), own(ns), ((rows, 512), lambda j, s: (0, j))],
        [((4096, 2 * rows), lambda j, s: (0, 0))], shaped((4096, 2 * rows)), tab,
        traffic=8 * rows * 4096, limit=STREAM,
    )(video, short, other)


def weight_quarter_kernel(tab, block, out):
    out[0] = block[...]


def weight_quarter(tab, w):
    return call(
        weight_quarter_kernel, "weight_quarter", (2,),
        [((64, 512), lambda j, s: (0, 2 * (2 * s[1] + j) + s[0]))],
        [((1, 64, 512), lambda j, s: (j, 0, 0))], shaped((2, 64, 512)), tab, traffic=4 * 64 * 1024,
    )(w)


def project_kernel(tab, *refs, parts, added):
    video, short, other = refs[:3]
    weights = refs[3 : 3 + parts]
    out_own, out_other = refs[-2:]
    nv = video.shape[0]
    step = pl.program_id(0)

    for k in range(parts):

        @pl.when(step == k)
        def _(k=k):
            w = weights[k][...]
            first = jnp.dot(video[...], w, preferred_element_type=F32)
            second = jnp.dot(short[...], w, preferred_element_type=F32)
            third = jnp.dot(other[...], w, preferred_element_type=F32)
            if k == 0 and added:
                before_own, before_other = refs[3 + parts : 5 + parts]
                out_own[:nv] = before_own[:nv] + first
                out_own[nv:] = before_own[nv:] + second
                out_other[...] = before_other[...] + third
            elif k == 0:
                out_own[:nv], out_own[nv:], out_other[...] = first, second, third
            else:
                out_own[:nv] += first
                out_own[nv:] += second
                out_other[...] += third


def project(tab, video, short, other, weights, before=()):
    nv, ns, parts = video.shape[0], short.shape[0], len(weights)
    rows = nv + ns
    own = lambda n: ((n, 512), lambda j, s: (0, 2 * s[1 + j] + s[0]))
    whole = lambda shape: (shape, lambda j, s: (0, 0))
    return call(
        functools.partial(project_kernel, parts=parts, added=len(before) > 0), "project", (parts,),
        [own(nv), own(ns), ((rows, 512), lambda j, s: (0, s[1 + j]))]
        + [whole((512, 768))] * parts + [whole((rows, 768))] * len(before),
        [whole((rows, 768))] * 2, [shaped((rows, 768), F32)] * 2, tab,
        flops=4 * rows * 512 * 768 * parts, traffic=parts * (512 * 768 * 2 + rows * 2048) + rows * 768 * 8,
        limit=STREAM,
    )(video, short, other, *weights, *before)


def spin(block, cosines, sines):
    return block * cosines + pltpu.roll(block, HEAD // 2, 1) * sines


def heads_kernel(near, near_got, far, far_got, bias, cosines, sines, queries, keys_values):
    total = near[...] + near_got[...] + far[...] + far_got[...] + bias[...]
    for h in range(QH):
        part = slice(h * HEAD, (h + 1) * HEAD)
        queries[:, part] = spin(total[:, part], cosines[...], sines[...]).astype(BF)
    keys_values[:, :HEAD] = spin(total[:, ATT : ATT + HEAD], cosines[...], sines[...]).astype(BF)
    keys_values[:, HEAD:] = total[:, ATT + HEAD :].astype(BF)


def heads(near, near_got, far, far_got, bias, cosines, sines):
    rows = near.shape[0]
    at = lambda i: (i, 0)
    big, small = ((128, 768), at), ((128, HEAD), at)
    return call(
        heads_kernel, "heads", (rows // 128,),
        [big, big, big, big, ((1, 768), lambda i: (0, 0)), small, small],
        [((128, ATT), at), ((128, 2 * HEAD), at)],
        [shaped((rows, ATT)), shaped((rows, 2 * HEAD))], traffic=rows * 768 * 18,
    )(near, near_got, far, far_got, bias, cosines, sines)


def stacked(block, count):
    return jnp.concatenate([block[:, h * HEAD : (h + 1) * HEAD] for h in range(count)], axis=0)


def attention_core(queries, keys, values, grad, allowed):
    nt = (((1,), (1,)), ((), ()))
    scores = lax.dot_general(queries, keys, nt, preferred_element_type=F32) * SCALE
    scores = jnp.where(allowed, scores, -1e30)
    peak = jnp.max(scores, axis=1, keepdims=True)
    weights = jnp.exp(scores - peak)
    probs = weights * (1.0 / jnp.sum(weights, axis=1, keepdims=True))
    probs_half = probs.astype(BF)
    attended = jnp.dot(probs_half, values, preferred_element_type=F32).astype(BF)
    deltas = jnp.sum(grad.astype(F32) * attended.astype(F32), axis=1, keepdims=True)
    dprob = lax.dot_general(grad, values, nt, preferred_element_type=F32)
    dscore = (probs * (dprob - deltas) * SCALE).astype(BF)
    dquery = jnp.dot(dscore, keys, preferred_element_type=F32)
    dkey = jnp.dot(queries.T, dscore, preferred_element_type=F32)
    dvalue = jnp.dot(grad.T, probs_half, preferred_element_type=F32)
    return attended, dquery, dkey, dvalue


def attention_kernel(tab, queries, keys_values, segments, ga, gb, cosines, sines, result, dkv, total, *, video):
    step = pl.program_id(0)
    n = queries.shape[0]
    m = keys_values.shape[0]
    query_at = lax.broadcasted_iota(jnp.int32, (n, m), 0)
    key_at = lax.broadcasted_iota(jnp.int32, (n, m), 1)
    if video:
        allowed = key_at <= query_at + tab[0]
    else:
        allowed = (segments[1] == segments[0][:, :1]) & (key_at <= query_at)
    allowed = jnp.concatenate([allowed, allowed], axis=0)
    grad = (ga[...] + gb[...]).astype(BF)
    attended, dquery, dkey, dvalue = attention_core(
        stacked(queries[...], 2), keys_values[:, :HEAD], keys_values[:, HEAD:], stacked(grad, 2), allowed
    )
    for h in range(2):
        part = slice(h * HEAD, (h + 1) * HEAD)
        result[0, :, part] = attended[h * n : (h + 1) * n]
        result[1, :, part] = spin(dquery[h * n : (h + 1) * n], cosines[...], -sines[...]).astype(BF)

    @pl.when(step == 0)
    def _():
        total[0] = dkey
        total[1] = dvalue

    @pl.when(step == 1)
    def _():
        dkey_all = (total[0] + dkey).T
        if not video:
            dkey_all = spin(dkey_all, cosines[...], -sines[...])
        dkv[:, :HEAD] = dkey_all.astype(BF)
        dkv[:, HEAD:] = (total[1] + dvalue).T.astype(BF)


def attention(video, first_row, start, count, queries, keys_values, segments, ga, gb, cosines, sines):
    m = keys_values.shape[0] if video else count
    n = count
    row = start
    pair = ((n, 2 * HEAD), lambda i, s: (row, i))
    angle = ((n, HEAD), lambda i, s: (row, 0))
    keys = ((m, 2 * HEAD), lambda i, s: (0 if video else row, 0))
    return call(
        functools.partial(attention_kernel, video=video), "video_attention" if video else "short_attention", (2,),
        [pair, keys, (segments.shape, lambda i, s: (0, 0, 0)), pair, pair, angle, angle],
        [((2, n, 2 * HEAD), lambda i, s: (0, 0, i)), ((m, 2 * HEAD), lambda i, s: (0, 0))],
        [shaped((2, n, ATT)), shaped((m, 2 * HEAD))], first_row,
        flops=2 * 5 * QH * n * m * HEAD, traffic=m * 1024, scratch=[pltpu.VMEM((2, HEAD, m), F32)], limit=48,
    )(queries, keys_values, segments, ga, gb, cosines, sines)


def collect_kernel(parts, cosines, sines, out):
    rows = out.shape[0]
    total = jnp.zeros((rows, 2 * HEAD), F32)
    for k in range(parts.shape[0]):
        total += parts[k].astype(F32)
    out[:, :HEAD] = spin(total[:, :HEAD], cosines[...], -sines[...]).astype(BF)
    out[:, HEAD:] = total[:, HEAD:].astype(BF)


def collect(parts, cosines, sines):
    count, rows = parts.shape[:2]
    zero = lambda i: (0, 0)
    return call(
        collect_kernel, "collect", (1,),
        [((count, rows, 2 * HEAD), lambda i: (0, 0, 0)), ((rows, HEAD), zero), ((rows, HEAD), zero)],
        [((rows, 2 * HEAD), zero)], shaped((rows, 2 * HEAD)), traffic=count * rows * 512,
    )(parts, cosines, sines)


W_BLOCK = ((1, 8, 1, 64, 512), lambda j, *s: (j // 2, 0, j % 2, 0, 0))


def whole_weights(ref):
    return ref[0, :, 0].reshape(ATT, 512)


def grad_attended_kernel(core_ref, video, short, other, w, total_own, total_other):
    nv = video.shape[0]

    @pl.when(pl.program_id(0) == 0)
    def _():
        total_own[...] = jnp.zeros_like(total_own)
        total_other[...] = jnp.zeros_like(total_other)

    block = whole_weights(w).T
    total_other[...] += jnp.dot(other[...], block, preferred_element_type=F32)
    total_own[:nv] += jnp.dot(video[...], block, preferred_element_type=F32)
    total_own[nv:] += jnp.dot(short[...], block, preferred_element_type=F32)


def grad_attended_parts(core, video, short, other, w):
    nv, ns = video.shape[0], short.shape[0]
    rows = nv + ns
    own = lambda n: ((n, 512), lambda j, s: (0, 2 * j + s[0]))
    out = ((rows, ATT), lambda j, s: (0, 0))
    return call(
        grad_attended_kernel, "grad_attended", (8,),
        [own(nv), own(ns), ((rows, 512), lambda j, s: (0, j)), W_BLOCK], [out, out],
        [shaped((rows, ATT), F32)] * 2, core, flops=4 * rows * 4096 * 512,
        traffic=rows * 16384 + 4096 * 1024, limit=STREAM,
    )(video, short, other, w)


def layer_out_kernel(tab, video_att, short_att, mine, theirs, video, short):
    for w, at in ((mine, tab[0]), (theirs, 1 - tab[0])):
        block = whole_weights(w)
        where = pl.ds(pl.multiple_of(at * 512, 512), 512)
        video[:, where] = jnp.dot(video_att[0], block, preferred_element_type=F32).astype(BF)
        short[:, where] = jnp.dot(short_att[0], block, preferred_element_type=F32).astype(BF)


def layer_out(tab, video_att, short_att, mine, theirs):
    nv, ns = video_att.shape[1], short_att.shape[1]
    att = lambda n: ((1, n, ATT), lambda j, s: (0, 0, 0))
    return call(
        layer_out_kernel, "layer_out", (8,), [att(nv), att(ns), W_BLOCK, W_BLOCK],
        [((nv, 1024), lambda j, s: (0, j)), ((ns, 1024), lambda j, s: (0, j))],
        [shaped((nv, 8192)), shaped((ns, 8192))], tab,
        flops=2 * (nv + ns) * 8192 * ATT, traffic=8192 * 1024 + (nv + ns) * 16384, limit=STREAM,
    )(video_att, short_att, mine, theirs)


TAIL = 16


def numbers(*entries):
    return jnp.stack([jnp.asarray(e, jnp.int32) for e in entries])


def turn_table(at):
    core, y = at["c"], at["yh"] * 2 + at["yl"]
    order = []
    for tz in range(4):
        for tyl in range(2):
            for tx in range(4):
                for tyh in range(2):
                    dy = (tyh * 2 + tyl - y + 4) % 4
                    order.append(jnp.where(core == 0, tz * 16 + tx * 4 + dy, tx * 16 + tz * 4 + dy))
    return numbers(core, *order)


def term_kernel(tab, cot, tokens, *refs):
    rights, got, out = refs[:4], refs[4:-1], refs[-1]
    right = jnp.concatenate([r[0] for r in rights], axis=0)

    def write(left):
        total = jnp.dot(left[...], right, preferred_element_type=F32)
        for ref in got:
            total += ref[0].astype(F32)
        out[0] = total.astype(BF)

    pl.when(pl.program_id(0) < 2)(lambda: write(cot))
    pl.when(pl.program_id(0) >= 2)(lambda: write(tokens))


def term(place, cot, tokens, rights, got=()):
    wide = cot.shape[1]
    at = lambda i, s: (i // 2, i % 2, 0)
    block = ((1, 512, ATT), at)
    return call(
        term_kernel, "term", (4,),
        [
            ((512, wide), lambda i, s: (2 * s[0] + jnp.minimum(i, 1), 0)),
            ((512, wide), lambda i, s: (2 * s[0] + jnp.maximum(i - 2, 0), 0)),
        ]
        + [((1, r.shape[1], ATT), lambda i, s: (i // 2, 0, 0)) for r in rights] + [block] * len(got),
        [block], shaped((2, 1024, ATT)), numbers(place % 4),
        flops=4 * wide * 1024 * ATT, traffic=4 * wide * 1024 + 4 * wide * ATT + 4096 * ATT, limit=STREAM,
    )(cot, tokens, *rights, *got)


def summed(own, got):
    return sum((g.astype(F32) for g in got), own).astype(BF)


def scatter(places, cot, tokens, rights, parts):
    got = [to_first(term(places[0] + far, cot, tokens, rights), far) for far in (2, 1, 3)]
    first = [f.reshape(2, 4, 256, ATT) for f in [term(places[0], cot, tokens, rights)] + got]

    def rows(far):
        place = (places[1] + far) % 4
        return sum(lax.dynamic_index_in_dim(f, place, 1, keepdims=False).astype(F32) for f in first)

    got = []
    for far in (2, 1, 3):
        chunk = rows(far).astype(BF)
        *first, chunk = lax.optimization_barrier((*first, chunk))
        got.append(to_second(chunk, far))
    *got, _ = lax.optimization_barrier((*got, parts))
    piece = lambda far: sum(
        (g[:, far * 64 : (far + 1) * 64].astype(F32) for g in got), rows(0)[:, far * 64 : (far + 1) * 64]
    )
    late = [to_y(piece(far).astype(BF), far) for far in (2, 1, 3)]
    return late, piece(0)


def tail_of(row):
    high = lax.reduce_precision(row, 8, 7)
    n = row.shape[1]
    return jnp.concatenate(
        [high.astype(BF), (row - high).astype(BF), jnp.zeros((TAIL - 6, n), BF)], axis=0
    )


def tail_sum(tails):
    return sum(t[:3].astype(F32) + t[3:6].astype(F32) for t in tails)


def key_term_kernel(tab, left, ga, gb, tail, out):
    right = jnp.concatenate([ga[...], gb[...]], axis=0)
    rows = left[:, :, 0].reshape(1024, left.shape[4])
    out[0, :1024] = jnp.dot(rows, right, preferred_element_type=F32).astype(BF)
    out[0, 1024:] = tail[...]


def key_term(y, left, ga, gb, tail):
    rows, n = ga.shape
    whole = lambda shape: (shape, lambda i, s: (0, 0))
    return call(
        key_term_kernel, "key_term", (4,),
        [
            ((4, 4, 1, 64, 2 * rows), lambda i, s: (0, 0, ((i % 2) * 2 + i // 2 - s[0] + 4) % 4, 0, 0)),
            whole((rows, n)), whole((rows, n)), whole((TAIL, n)),
        ],
        [((1, 1024 + TAIL, n), lambda i, s: (i, 0, 0))], shaped((4, 1024 + TAIL, n)), numbers(y),
        flops=4 * rows * 4096 * n, traffic=4096 * (4 * rows + 2 * n), limit=STREAM,
    )(left.reshape(4, 4, 4, 64, 2 * rows), ga, gb, tail)


LATE_GROUPS = [
    [device_index(a, y, 0, b) if c == 0 else device_index(b, y, 1, a) for a in range(4) for b in range(4)]
    for c in range(2)
    for y in range(4)
]


def key_parts(terms):
    first = jnp.sum(terms[:, :1024].astype(F32), axis=0).astype(BF).reshape(16, 64, 256)
    tail = tail_of(tail_sum([terms[k, 1024:] for k in range(4)]))
    return jnp.concatenate([first, jnp.broadcast_to(tail[None], (16, TAIL, 256))], axis=1)


def key_sum(parts):
    parts = lax.all_to_all(parts, AXES, 0, 0, tiled=True, axis_index_groups=LATE_GROUPS)
    total = jnp.sum(parts.astype(F32), axis=0)
    return total[:64], total[64:67] + total[67:70]


def rope_angles(positions):
    half_dim = HEAD // 2
    freq_index = jnp.arange(half_dim, dtype=jnp.int32)
    inv_freq = jnp.exp(freq_index.astype(F32) * (-2.0 * THETA_LOG / HEAD))
    first_cut = HEAD // 8
    second_cut = first_cut + 3 * HEAD // 16
    pos_float = positions.astype(F32)
    chosen_pos = jnp.where(
        (freq_index < first_cut)[None, :],
        pos_float[0][:, None],
        jnp.where((freq_index < second_cut)[None, :], pos_float[1][:, None], pos_float[2][:, None]),
    )
    angles = chosen_pos * inv_freq[None, :]
    cosines, sines = jnp.cos(angles), jnp.sin(angles)
    return (
        jnp.concatenate([cosines, cosines], axis=1),
        jnp.concatenate([-sines, sines], axis=1),
    )


def to_all(value, axes, count):
    return lax.all_to_all(jnp.broadcast_to(value[None], (count,) + value.shape), axes, 0, 0)


def after(value, *others):
    return lax.optimization_barrier((value,) + others)[0]


def per_device(
    w_qkv, qkv_bias, w_out, video_x, video_pos, short_x, short_pos, short_seg, video_cot, short_cot
):
    at = {name: lax.axis_index(name) for name in AXES}
    core = numbers(at["c"])
    order = turn_table(at)
    nv, ns = video_x.shape[1], short_x.shape[1]
    rows = nv + ns
    video_x, short_x, video_cot, short_cot = video_x[0], short_x[0], video_cot[0], short_cot[0]

    mine = lax.dynamic_slice(w_qkv, (at["c"] * 512, 0), (512, 768))
    x_other = other_core(halves(1 - core, video_x, short_x))
    x_turned = turned(order, video_x, short_x, x_other)
    quarters = to_all(weight_quarter(numbers(at["c"], at["z"]), w_out), DP, 8)
    wide, later_cot, x_turned = lax.optimization_barrier(
        (jnp.broadcast_to(quarters[None], (4,) + quarters.shape), video_cot, x_turned)
    )
    wo = lax.all_to_all(wide, ("z",), 0, 0)
    first, third, facing, x_turned, x_other, c_send = lax.optimization_barrier((
        to_x(mine, 1), to_x(mine, 3), across(mine), x_turned, x_other,
        halves(1 - core, later_cot, short_cot),
    ))
    c_other = other_core(c_send)
    relay = lambda near: jnp.where(at["c"] == 0, facing, near)
    shard = lambda step, yh: ((at["x"] - step + 4) % 4) * 2 + yh
    near, off = at["yh"], 1 - at["yh"]
    part = project(
        numbers(at["c"], shard(0, near), shard(1, near), shard(3, near), shard(0, off)),
        video_x, short_x, x_other, [mine, first, third, facing],
    )
    far_first, far_third, second, c_turned, part = lax.optimization_barrier((
        to_x_or_across(relay(first), 1), to_x_or_across(relay(third), 3), to_x(mine, 2),
        turned(order, video_cot, short_cot, c_other), part,
    ))
    near_own, near_other = project(
        numbers(at["c"], shard(2, near), shard(1, off), shard(3, off)),
        video_x, short_x, x_other, [second, far_first, far_third], part,
    )
    far_second, near_own, near_other = lax.optimization_barrier(
        (to_x_or_across(relay(second), 2), near_own, near_other)
    )

    places = jnp.concatenate([video_pos[:, 0, :], short_pos[:, 0, :]], axis=1)
    cosines, sines = rope_angles(places)
    near_other = other_core(near_other)
    far_own, far_other = project(numbers(at["c"], shard(2, off)), video_x, short_x, x_other, [far_second])
    queries, keys_values = heads(
        near_own, near_other, far_own, other_core(far_other), qkv_bias[None], cosines, sines
    )
    wide = jnp.broadcast_to(keys_values[:nv][None], (16, nv, 2 * HEAD))
    wide, wo = lax.optimization_barrier((wide, wo))
    group = lax.all_to_all(wide, GRP, 0, 0).reshape(16 * nv, 2 * HEAD)

    wo_other = other_core(wo)
    grad_own, grad_other = grad_attended_parts(core, video_cot, short_cot, c_other, wo)
    grad_other = other_core(grad_other)

    segment = short_seg[0]
    segments = jnp.stack([jnp.broadcast_to(segment[:, None], (ns, ns)), jnp.broadcast_to(segment[None, :], (ns, ns))])
    first_row = ((at["z"] * 2 + at["yl"]) * 2 + at["c"]) * nv
    cut = lambda a: a[nv:]
    short_result, short_dkv = attention(
        False, numbers(0), 0, ns, cut(queries), cut(keys_values), segments, cut(grad_own), cut(grad_other),
        cut(cosines), cut(sines),
    )
    group, wo_other = lax.optimization_barrier((group, wo_other))
    video_result, video_dkv = attention(
        True, numbers(first_row), 0, nv, queries, group, jnp.zeros((1, 8, 128), jnp.int32), grad_own, grad_other,
        cosines, sines,
    )
    arrived = lax.all_to_all(video_dkv.reshape(16, nv, 2 * HEAD), GRP, 0, 0, tiled=True)

    results = (video_result, short_result, other_core(video_result), other_core(short_result))
    place = jnp.where(at["c"] == 0, at["z"], at["x"])
    second_place = jnp.where(at["c"] == 0, at["x"], at["z"])

    video_dkv = collect(arrived, cosines[:nv], sines[:nv])
    dkv = jnp.concatenate([video_dkv, short_dkv], axis=0)
    dkv_other = other_core(dkv)
    sum_q = sum(jnp.sum(r[1].astype(F32), axis=0) for r in results).reshape(2, 256)
    sum_kv = jnp.sum(dkv.astype(F32) + dkv_other.astype(F32), axis=0)[None]
    terms = key_term(at["yh"] * 2 + at["yl"], x_turned, dkv, dkv_other, tail_of(jnp.concatenate([sum_q, sum_kv], axis=0)))
    video_y, short_y = layer_out(core, after(video_result, terms), short_result, wo, wo_other)
    terms, video_y, short_y = lax.optimization_barrier(
        (lax.all_to_all(terms, ("yl", "yh"), 0, 0, tiled=True), video_y, short_y)
    )
    parts = key_parts(terms)
    late, own = scatter((place, second_place), c_turned, x_turned, results, parts)
    grad_kv, bias = key_sum(parts)
    grad_kv, bias, own, *late = lax.optimization_barrier((grad_kv, bias, own, *late))
    grad_out, grad_q = sum((g.astype(F32) for g in late), own)
    return (
        video_y[None],
        short_y[None],
        jnp.concatenate([grad_q, grad_kv], axis=1),
        grad_out.T,
        bias.reshape(768),
    )


def solution(mesh):
    fine = Mesh(mesh.devices.reshape(SIZES), AXES)
    return jax.shard_map(
        per_device,
        mesh=fine,
        in_specs=(
            P(DP, None),
            P(),
            P(DP, None),
            P(DP, GRP, None),
            P(None, DP, GRP),
            P(DP + GRP, None, None),
            P(None, DP + GRP, None),
            P(DP + GRP, None),
            P(DP, GRP, None),
            P(DP + GRP, None, None),
        ),
        out_specs=(
            P(DP, GRP, None),
            P(DP + GRP, None, None),
            P(GRP + DP, None),
            P(None, GRP + DP),
            P(),
        ),
        check_vma=False,
    )
```

```python
import functools

import jax
import jax.numpy as jnp
from jax import lax
from jax.experimental import pallas as pl
from jax.experimental.pallas import tpu as pltpu
from jax.sharding import Mesh
from jax.sharding import PartitionSpec as P

HEAD = 128
QH = 4
ATT = QH * HEAD
SCALE = HEAD ** (-0.5)
AXES = ("z", "yl", "c", "x", "yh")
SIZES = (4, 2, 2, 4, 2)
GRP = ("z", "yl", "c")
DP = ("x", "yh")
BF = jnp.bfloat16
F32 = jnp.float32
THETA_LOG = 13.815510557964274
STREAM = 52


def device_index(z, y, c, x):
    z, y, c, x = z % 4, y % 4, c % 2, x % 4
    return (((z * 2 + y % 2) * 2 + c) * 4 + x) * 2 + y // 2


def pairs(target):
    result = []
    for z in range(4):
        for y in range(4):
            for c in range(2):
                for x in range(4):
                    result.append((device_index(z, y, c, x), device_index(*target(z, y, c, x))))
    return result


def move(value, target):
    return lax.ppermute(value, AXES, pairs(target))


def other_core(value):
    return move(value, lambda z, y, c, x: (z, y, c + 1, x))


def to_x(value, step):
    return move(value, lambda z, y, c, x: (z, y, c, x + step))


def to_z(value, step):
    return move(value, lambda z, y, c, x: (z + step, y, c, x))


def to_y(value, step):
    return move(value, lambda z, y, c, x: (z, y + step, c, x))


def across(value):
    return move(value, lambda z, y, c, x: (z, 3 - y, c, x))


def to_x_or_across(value, step):
    return move(
        value, lambda z, y, c, x: (z, y, c, x + step) if c == 0 else (z, 3 - y, c, x)
    )


def to_first(value, step):
    return move(
        value, lambda z, y, c, x: (z + step, y, c, x) if c == 0 else (z, y, c, x + step)
    )


def to_second(value, step):
    return move(
        value, lambda z, y, c, x: (z, y, c, x + step) if c == 0 else (z + step, y, c, x)
    )


def call(kernel, name, grid, ins, outs, shapes, tab=None, flops=0, traffic=0, scratch=(), limit=24):
    spec = lambda pair: pl.BlockSpec(*pair)
    single = not isinstance(shapes, list)
    in_specs = [spec(i) for i in ins]
    out_specs = spec(outs[0]) if single else [spec(o) for o in outs]
    cost = pl.CostEstimate(flops=flops, bytes_accessed=traffic, transcendentals=0)
    options = dict(
        out_shape=shapes,
        compiler_params=pltpu.CompilerParams(vmem_limit_bytes=limit * 1024 * 1024),
        cost_estimate=cost,
        name=name,
    )
    if tab is None:
        return pl.pallas_call(
            kernel, grid=grid, in_specs=in_specs, out_specs=out_specs, scratch_shapes=scratch, **options
        )
    grid_spec = pltpu.PrefetchScalarGridSpec(
        num_scalar_prefetch=1, grid=grid, in_specs=in_specs, out_specs=out_specs, scratch_shapes=scratch
    )
    return functools.partial(pl.pallas_call(kernel, grid_spec=grid_spec, **options), tab)


def shaped(shape, kind=BF):
    return jax.ShapeDtypeStruct(shape, kind)


def halves_kernel(core_ref, *refs):
    out = refs[4]
    n = refs[0].shape[0]
    for k in range(2):
        out[:n, k * 512 : (k + 1) * 512] = refs[k][...]
        out[n:, k * 512 : (k + 1) * 512] = refs[2 + k][...]


def halves(core, video, short):
    nv, ns = video.shape[0], short.shape[0]
    theirs = lambda n, k: ((n, 512), lambda j, s: (0, 4 * j + 2 * k + s[0]))
    return call(
        halves_kernel, "halves", (4,), [theirs(nv, 0), theirs(nv, 1), theirs(ns, 0), theirs(ns, 1)],
        [((nv + ns, 1024), lambda j, s: (0, j))], shaped((nv + ns, 4096)), core,
        traffic=4 * (nv + ns) * 4096, limit=STREAM,
    )(video, video, short, short)


def turn_kernel(tab, video, short, other, out):
    nv, rows = video.shape[0], other.shape[0]
    step = pl.program_id(0)
    first, second, third = video[...].T, short[...].T, other[...].T
    for k in range(8):
        where = pl.ds(pl.multiple_of(tab[1 + step * 8 + k] * 64, 64), 64)
        out[where, :nv] = first[k * 64 : (k + 1) * 64]
        out[where, nv:rows] = second[k * 64 : (k + 1) * 64]
        out[where, rows:] = third[k * 64 : (k + 1) * 64]


def turned(tab, video, short, other):
    nv, ns = video.shape[0], short.shape[0]
    rows = nv + ns
    own = lambda n: ((n, 512), lambda j, s: (0, 2 * j + s[0]))
    return call(
        turn_kernel, "turned", (8,),
        [own(nv), own(ns), ((rows, 512), lambda j, s: (0, j))],
        [((4096, 2 * rows), lambda j, s: (0, 0))], shaped((4096, 2 * rows)), tab,
        traffic=8 * rows * 4096, limit=STREAM,
    )(video, short, other)


def weight_quarter_kernel(tab, block, out):
    out[0] = block[...]


def weight_quarter(tab, w):
    return call(
        weight_quarter_kernel, "weight_quarter", (2,),
        [((64, 512), lambda j, s: (0, 2 * (2 * s[1] + j) + s[0]))],
        [((1, 64, 512), lambda j, s: (j, 0, 0))], shaped((2, 64, 512)), tab, traffic=4 * 64 * 1024,
    )(w)


def project_kernel(tab, *refs, parts, added):
    video, short, other = refs[:3]
    weights = refs[3 : 3 + parts]
    out_own, out_other = refs[-2:]
    nv = video.shape[0]
    step = pl.program_id(0)

    for k in range(parts):

        @pl.when(step == k)
        def _(k=k):
            w = weights[k][...]
            first = jnp.dot(video[...], w, preferred_element_type=F32)
            second = jnp.dot(short[...], w, preferred_element_type=F32)
            third = jnp.dot(other[...], w, preferred_element_type=F32)
            if k == 0 and added:
                before_own, before_other = refs[3 + parts : 5 + parts]
                out_own[:nv] = before_own[:nv] + first
                out_own[nv:] = before_own[nv:] + second
                out_other[...] = before_other[...] + third
            elif k == 0:
                out_own[:nv], out_own[nv:], out_other[...] = first, second, third
            else:
                out_own[:nv] += first
                out_own[nv:] += second
                out_other[...] += third


def project(tab, video, short, other, weights, before=()):
    nv, ns, parts = video.shape[0], short.shape[0], len(weights)
    rows = nv + ns
    own = lambda n: ((n, 512), lambda j, s: (0, 2 * s[1 + j] + s[0]))
    whole = lambda shape: (shape, lambda j, s: (0, 0))
    return call(
        functools.partial(project_kernel, parts=parts, added=len(before) > 0), "project", (parts,),
        [own(nv), own(ns), ((rows, 512), lambda j, s: (0, s[1 + j]))]
        + [whole((512, 768))] * parts + [whole((rows, 768))] * len(before),
        [whole((rows, 768))] * 2, [shaped((rows, 768), F32)] * 2, tab,
        flops=4 * rows * 512 * 768 * parts, traffic=parts * (512 * 768 * 2 + rows * 2048) + rows * 768 * 8,
        limit=STREAM,
    )(video, short, other, *weights, *before)


def spin(block, cosines, sines):
    return block * cosines + pltpu.roll(block, HEAD // 2, 1) * sines


def heads_kernel(near, near_got, far, far_got, bias, cosines, sines, queries, keys_values):
    total = near[...] + near_got[...] + far[...] + far_got[...] + bias[...]
    for h in range(QH):
        part = slice(h * HEAD, (h + 1) * HEAD)
        queries[:, part] = spin(total[:, part], cosines[...], sines[...]).astype(BF)
    keys_values[:, :HEAD] = spin(total[:, ATT : ATT + HEAD], cosines[...], sines[...]).astype(BF)
    keys_values[:, HEAD:] = total[:, ATT + HEAD :].astype(BF)


def heads(near, near_got, far, far_got, bias, cosines, sines):
    rows = near.shape[0]
    at = lambda i: (i, 0)
    big, small = ((128, 768), at), ((128, HEAD), at)
    return call(
        heads_kernel, "heads", (rows // 128,),
        [big, big, big, big, ((1, 768), lambda i: (0, 0)), small, small],
        [((128, ATT), at), ((128, 2 * HEAD), at)],
        [shaped((rows, ATT)), shaped((rows, 2 * HEAD))], traffic=rows * 768 * 18,
    )(near, near_got, far, far_got, bias, cosines, sines)


def stacked(block, count):
    return jnp.concatenate([block[:, h * HEAD : (h + 1) * HEAD] for h in range(count)], axis=0)


def attention_core(queries, keys, values, grad, allowed):
    nt = (((1,), (1,)), ((), ()))
    scores = lax.dot_general(queries, keys, nt, preferred_element_type=F32) * SCALE
    scores = jnp.where(allowed, scores, -1e30)
    peak = jnp.max(scores, axis=1, keepdims=True)
    weights = jnp.exp(scores - peak)
    probs = weights * (1.0 / jnp.sum(weights, axis=1, keepdims=True))
    probs_half = probs.astype(BF)
    attended = jnp.dot(probs_half, values, preferred_element_type=F32).astype(BF)
    deltas = jnp.sum(grad.astype(F32) * attended.astype(F32), axis=1, keepdims=True)
    dprob = lax.dot_general(grad, values, nt, preferred_element_type=F32)
    dscore = (probs * (dprob - deltas) * SCALE).astype(BF)
    dquery = jnp.dot(dscore, keys, preferred_element_type=F32)
    dkey = jnp.dot(queries.T, dscore, preferred_element_type=F32)
    dvalue = jnp.dot(grad.T, probs_half, preferred_element_type=F32)
    return attended, dquery, dkey, dvalue


def attention_kernel(tab, queries, keys_values, segments, ga, gb, cosines, sines, result, dkv, total, *, video):
    step = pl.program_id(0)
    n = queries.shape[0]
    m = keys_values.shape[0]
    query_at = lax.broadcasted_iota(jnp.int32, (n, m), 0)
    key_at = lax.broadcasted_iota(jnp.int32, (n, m), 1)
    if video:
        allowed = key_at <= query_at + tab[0]
    else:
        allowed = (segments[1] == segments[0][:, :1]) & (key_at <= query_at)
    allowed = jnp.concatenate([allowed, allowed], axis=0)
    grad = (ga[...] + gb[...]).astype(BF)
    attended, dquery, dkey, dvalue = attention_core(
        stacked(queries[...], 2), keys_values[:, :HEAD], keys_values[:, HEAD:], stacked(grad, 2), allowed
    )
    for h in range(2):
        part = slice(h * HEAD, (h + 1) * HEAD)
        result[0, :, part] = attended[h * n : (h + 1) * n]
        result[1, :, part] = spin(dquery[h * n : (h + 1) * n], cosines[...], -sines[...]).astype(BF)

    @pl.when(step == 0)
    def _():
        total[0] = dkey
        total[1] = dvalue

    @pl.when(step == 1)
    def _():
        dkey_all = (total[0] + dkey).T
        if not video:
            dkey_all = spin(dkey_all, cosines[...], -sines[...])
        dkv[:, :HEAD] = dkey_all.astype(BF)
        dkv[:, HEAD:] = (total[1] + dvalue).T.astype(BF)


def attention(video, first_row, start, count, queries, keys_values, segments, ga, gb, cosines, sines):
    m = keys_values.shape[0] if video else count
    n = count
    row = start
    pair = ((n, 2 * HEAD), lambda i, s: (row, i))
    angle = ((n, HEAD), lambda i, s: (row, 0))
    keys = ((m, 2 * HEAD), lambda i, s: (0 if video else row, 0))
    return call(
        functools.partial(attention_kernel, video=video), "video_attention" if video else "short_attention", (2,),
        [pair, keys, (segments.shape, lambda i, s: (0, 0, 0)), pair, pair, angle, angle],
        [((2, n, 2 * HEAD), lambda i, s: (0, 0, i)), ((m, 2 * HEAD), lambda i, s: (0, 0))],
        [shaped((2, n, ATT)), shaped((m, 2 * HEAD))], first_row,
        flops=2 * 5 * QH * n * m * HEAD, traffic=m * 1024, scratch=[pltpu.VMEM((2, HEAD, m), F32)], limit=48,
    )(queries, keys_values, segments, ga, gb, cosines, sines)


def collect_kernel(parts, cosines, sines, out):
    rows = out.shape[0]
    total = jnp.zeros((rows, 2 * HEAD), F32)
    for k in range(parts.shape[0]):
        total += parts[k].astype(F32)
    out[:, :HEAD] = spin(total[:, :HEAD], cosines[...], -sines[...]).astype(BF)
    out[:, HEAD:] = total[:, HEAD:].astype(BF)


def collect(parts, cosines, sines):
    count, rows = parts.shape[:2]
    zero = lambda i: (0, 0)
    return call(
        collect_kernel, "collect", (1,),
        [((count, rows, 2 * HEAD), lambda i: (0, 0, 0)), ((rows, HEAD), zero), ((rows, HEAD), zero)],
        [((rows, 2 * HEAD), zero)], shaped((rows, 2 * HEAD)), traffic=count * rows * 512,
    )(parts, cosines, sines)


W_BLOCK = ((1, 8, 1, 64, 512), lambda j, *s: (j // 2, 0, j % 2, 0, 0))


def whole_weights(ref):
    return ref[0, :, 0].reshape(ATT, 512)


def grad_attended_kernel(core_ref, video, short, other, w, total_own, sent, total_other):
    nv = video.shape[0]

    @pl.when(pl.program_id(0) == 0)
    def _():
        total_own[...] = jnp.zeros_like(total_own)
        total_other[...] = jnp.zeros_like(total_other)

    block = whole_weights(w).T
    total_other[...] += jnp.dot(other[...], block, preferred_element_type=F32)
    total_own[:nv] += jnp.dot(video[...], block, preferred_element_type=F32)
    total_own[nv:] += jnp.dot(short[...], block, preferred_element_type=F32)

    @pl.when(pl.program_id(0) == pl.num_programs(0) - 1)
    def _():
        sent[...] = total_other[...].astype(BF)


def grad_attended_parts(core, video, short, other, w):
    nv, ns = video.shape[0], short.shape[0]
    rows = nv + ns
    own = lambda n: ((n, 512), lambda j, s: (0, 2 * j + s[0]))
    out = ((rows, ATT), lambda j, s: (0, 0))
    return call(
        grad_attended_kernel, "grad_attended", (8,),
        [own(nv), own(ns), ((rows, 512), lambda j, s: (0, j)), W_BLOCK], [out, out],
        [shaped((rows, ATT), F32), shaped((rows, ATT))], core, flops=4 * rows * 4096 * 512,
        scratch=[pltpu.VMEM((rows, ATT), F32)],
        traffic=rows * 16384 + 4096 * 1024, limit=STREAM,
    )(video, short, other, w)


def layer_out_kernel(tab, video_att, short_att, mine, theirs, video, short):
    for w, at in ((mine, tab[0]), (theirs, 1 - tab[0])):
        block = whole_weights(w)
        where = pl.ds(pl.multiple_of(at * 512, 512), 512)
        video[:, where] = jnp.dot(video_att[0], block, preferred_element_type=F32).astype(BF)
        short[:, where] = jnp.dot(short_att[0], block, preferred_element_type=F32).astype(BF)


def layer_out(tab, video_att, short_att, mine, theirs):
    nv, ns = video_att.shape[1], short_att.shape[1]
    att = lambda n: ((1, n, ATT), lambda j, s: (0, 0, 0))
    return call(
        layer_out_kernel, "layer_out", (8,), [att(nv), att(ns), W_BLOCK, W_BLOCK],
        [((nv, 1024), lambda j, s: (0, j)), ((ns, 1024), lambda j, s: (0, j))],
        [shaped((nv, 8192)), shaped((ns, 8192))], tab,
        flops=2 * (nv + ns) * 8192 * ATT, traffic=8192 * 1024 + (nv + ns) * 16384, limit=STREAM,
    )(video_att, short_att, mine, theirs)


TAIL = 16


def numbers(*entries):
    return jnp.stack([jnp.asarray(e, jnp.int32) for e in entries])


def turn_table(at):
    core, y = at["c"], at["yh"] * 2 + at["yl"]
    order = []
    for tz in range(4):
        for tyl in range(2):
            for tx in range(4):
                for tyh in range(2):
                    dy = (tyh * 2 + tyl - y + 4) % 4
                    order.append(jnp.where(core == 0, tz * 16 + tx * 4 + dy, tx * 16 + tz * 4 + dy))
    return numbers(core, *order)


def term_kernel(tab, cot, tokens, *refs):
    rights, got, out = refs[:4], refs[4:-1], refs[-1]
    right = jnp.concatenate([r[0] for r in rights], axis=0)

    def write(left):
        total = jnp.dot(left[...], right, preferred_element_type=F32)
        for ref in got:
            total += ref[0].astype(F32)
        out[0] = total.astype(BF)

    pl.when(pl.program_id(0) < 2)(lambda: write(cot))
    pl.when(pl.program_id(0) >= 2)(lambda: write(tokens))


def term(place, cot, tokens, rights, got=()):
    wide = cot.shape[1]
    at = lambda i, s: (i // 2, i % 2, 0)
    block = ((1, 512, ATT), at)
    return call(
        term_kernel, "term", (4,),
        [
            ((512, wide), lambda i, s: (2 * s[0] + jnp.minimum(i, 1), 0)),
            ((512, wide), lambda i, s: (2 * s[0] + jnp.maximum(i - 2, 0), 0)),
        ]
        + [((1, r.shape[1], ATT), lambda i, s: (i // 2, 0, 0)) for r in rights] + [block] * len(got),
        [block], shaped((2, 1024, ATT)), numbers(place % 4),
        flops=4 * wide * 1024 * ATT, traffic=4 * wide * 1024 + 4 * wide * ATT + 4096 * ATT, limit=STREAM,
    )(cot, tokens, *rights, *got)


def summed(own, got):
    return sum((g.astype(F32) for g in got), own).astype(BF)


def scatter(places, cot, tokens, rights, parts):
    got = [to_first(term(places[0] + far, cot, tokens, rights), far) for far in (2, 1, 3)]
    first = [f.reshape(2, 4, 256, ATT) for f in [term(places[0], cot, tokens, rights)] + got]

    def rows(far):
        place = (places[1] + far) % 4
        return sum(lax.dynamic_index_in_dim(f, place, 1, keepdims=False).astype(F32) for f in first)

    got = []
    for far in (2, 1, 3):
        chunk = rows(far).astype(BF)
        *first, chunk = lax.optimization_barrier((*first, chunk))
        got.append(to_second(chunk, far))
    *got, _ = lax.optimization_barrier((*got, parts))
    piece = lambda far: sum(
        (g[:, far * 64 : (far + 1) * 64].astype(F32) for g in got), rows(0)[:, far * 64 : (far + 1) * 64]
    )
    late = [to_y(piece(far).astype(BF), far) for far in (2, 1, 3)]
    return late, piece(0)


def tail_of(row):
    high = lax.reduce_precision(row, 8, 7)
    n = row.shape[1]
    return jnp.concatenate(
        [high.astype(BF), (row - high).astype(BF), jnp.zeros((TAIL - 6, n), BF)], axis=0
    )


def tail_sum(tails):
    return sum(t[:3].astype(F32) + t[3:6].astype(F32) for t in tails)


def key_term_kernel(tab, left, ga, gb, tail, out):
    right = jnp.concatenate([ga[...], gb[...]], axis=0)
    rows = left[:, :, 0].reshape(1024, left.shape[4])
    out[0, :1024] = jnp.dot(rows, right, preferred_element_type=F32).astype(BF)
    out[0, 1024:] = tail[...]


def key_term(y, left, ga, gb, tail):
    rows, n = ga.shape
    whole = lambda shape: (shape, lambda i, s: (0, 0))
    return call(
        key_term_kernel, "key_term", (4,),
        [
            ((4, 4, 1, 64, 2 * rows), lambda i, s: (0, 0, ((i % 2) * 2 + i // 2 - s[0] + 4) % 4, 0, 0)),
            whole((rows, n)), whole((rows, n)), whole((TAIL, n)),
        ],
        [((1, 1024 + TAIL, n), lambda i, s: (i, 0, 0))], shaped((4, 1024 + TAIL, n)), numbers(y),
        flops=4 * rows * 4096 * n, traffic=4096 * (4 * rows + 2 * n), limit=STREAM,
    )(left.reshape(4, 4, 4, 64, 2 * rows), ga, gb, tail)


LATE_GROUPS = [
    [device_index(a, y, 0, b) if c == 0 else device_index(b, y, 1, a) for a in range(4) for b in range(4)]
    for c in range(2)
    for y in range(4)
]


def key_parts(terms):
    first = jnp.sum(terms[:, :1024].astype(F32), axis=0).astype(BF).reshape(16, 64, 256)
    tail = tail_of(tail_sum([terms[k, 1024:] for k in range(4)]))
    return jnp.concatenate([first, jnp.broadcast_to(tail[None], (16, TAIL, 256))], axis=1)


def key_sum(parts):
    parts = lax.all_to_all(parts, AXES, 0, 0, tiled=True, axis_index_groups=LATE_GROUPS)
    total = jnp.sum(parts.astype(F32), axis=0)
    return total[:64], total[64:67] + total[67:70]


def rope_angles(positions):
    half_dim = HEAD // 2
    freq_index = jnp.arange(half_dim, dtype=jnp.int32)
    inv_freq = jnp.exp(freq_index.astype(F32) * (-2.0 * THETA_LOG / HEAD))
    first_cut = HEAD // 8
    second_cut = first_cut + 3 * HEAD // 16
    pos_float = positions.astype(F32)
    chosen_pos = jnp.where(
        (freq_index < first_cut)[None, :],
        pos_float[0][:, None],
        jnp.where((freq_index < second_cut)[None, :], pos_float[1][:, None], pos_float[2][:, None]),
    )
    angles = chosen_pos * inv_freq[None, :]
    cosines, sines = jnp.cos(angles), jnp.sin(angles)
    return (
        jnp.concatenate([cosines, cosines], axis=1),
        jnp.concatenate([-sines, sines], axis=1),
    )


def to_all(value, axes, count):
    return lax.all_to_all(jnp.broadcast_to(value[None], (count,) + value.shape), axes, 0, 0)


def after(value, *others):
    return lax.optimization_barrier((value,) + others)[0]


def per_device(
    w_qkv, qkv_bias, w_out, video_x, video_pos, short_x, short_pos, short_seg, video_cot, short_cot
):
    at = {name: lax.axis_index(name) for name in AXES}
    core = numbers(at["c"])
    order = turn_table(at)
    nv, ns = video_x.shape[1], short_x.shape[1]
    rows = nv + ns
    video_x, short_x, video_cot, short_cot = video_x[0], short_x[0], video_cot[0], short_cot[0]

    mine = lax.dynamic_slice(w_qkv, (at["c"] * 512, 0), (512, 768))
    x_other = other_core(halves(1 - core, video_x, short_x))
    x_turned = turned(order, video_x, short_x, x_other)
    quarters = to_all(weight_quarter(numbers(at["c"], at["z"]), w_out), DP, 8)
    wide, later_cot, x_turned = lax.optimization_barrier(
        (jnp.broadcast_to(quarters[None], (4,) + quarters.shape), video_cot, x_turned)
    )
    wo = lax.all_to_all(wide, ("z",), 0, 0)
    first, third, facing, x_turned, x_other, c_send = lax.optimization_barrier((
        to_x(mine, 1), to_x(mine, 3), across(mine), x_turned, x_other,
        halves(1 - core, later_cot, short_cot),
    ))
    c_other = other_core(c_send)
    relay = lambda near: jnp.where(at["c"] == 0, facing, near)
    shard = lambda step, yh: ((at["x"] - step + 4) % 4) * 2 + yh
    near, off = at["yh"], 1 - at["yh"]
    part = project(
        numbers(at["c"], shard(0, near), shard(1, near), shard(3, near), shard(0, off)),
        video_x, short_x, x_other, [mine, first, third, facing],
    )
    far_first, far_third, second, c_turned, part = lax.optimization_barrier((
        to_x_or_across(relay(first), 1), to_x_or_across(relay(third), 3), to_x(mine, 2),
        turned(order, video_cot, short_cot, c_other), part,
    ))
    near_own, near_other = project(
        numbers(at["c"], shard(2, near), shard(1, off), shard(3, off)),
        video_x, short_x, x_other, [second, far_first, far_third], part,
    )
    far_second, near_own, near_other = lax.optimization_barrier(
        (to_x_or_across(relay(second), 2), near_own, near_other)
    )

    places = jnp.concatenate([video_pos[:, 0, :], short_pos[:, 0, :]], axis=1)
    cosines, sines = rope_angles(places)
    near_other = other_core(near_other)
    far_own, far_other = project(numbers(at["c"], shard(2, off)), video_x, short_x, x_other, [far_second])
    queries, keys_values = heads(
        near_own, near_other, far_own, other_core(far_other), qkv_bias[None], cosines, sines
    )
    wide = jnp.broadcast_to(keys_values[:nv][None], (16, nv, 2 * HEAD))
    wide, wo = lax.optimization_barrier((wide, wo))
    group = lax.all_to_all(wide, GRP, 0, 0).reshape(16 * nv, 2 * HEAD)

    wo_other = other_core(wo)
    grad_own, grad_other = grad_attended_parts(core, video_cot, short_cot, c_other, wo)
    grad_other = other_core(grad_other)

    segment = short_seg[0]
    segments = jnp.stack([jnp.broadcast_to(segment[:, None], (ns, ns)), jnp.broadcast_to(segment[None, :], (ns, ns))])
    first_row = ((at["z"] * 2 + at["yl"]) * 2 + at["c"]) * nv
    cut = lambda a: a[nv:]
    short_result, short_dkv = attention(
        False, numbers(0), 0, ns, cut(queries), cut(keys_values), segments, cut(grad_own), cut(grad_other),
        cut(cosines), cut(sines),
    )
    group, wo_other = lax.optimization_barrier((group, wo_other))
    video_result, video_dkv = attention(
        True, numbers(first_row), 0, nv, queries, group, jnp.zeros((1, 8, 128), jnp.int32), grad_own, grad_other,
        cosines, sines,
    )
    arrived = lax.all_to_all(video_dkv.reshape(16, nv, 2 * HEAD), GRP, 0, 0, tiled=True)

    results = (video_result, short_result, other_core(video_result), other_core(short_result))
    place = jnp.where(at["c"] == 0, at["z"], at["x"])
    second_place = jnp.where(at["c"] == 0, at["x"], at["z"])

    video_dkv = collect(arrived, cosines[:nv], sines[:nv])
    dkv = jnp.concatenate([video_dkv, short_dkv], axis=0)
    dkv_other = other_core(dkv)
    sum_q = sum(jnp.sum(r[1].astype(F32), axis=0) for r in results).reshape(2, 256)
    sum_kv = jnp.sum(dkv.astype(F32) + dkv_other.astype(F32), axis=0)[None]
    terms = key_term(at["yh"] * 2 + at["yl"], x_turned, dkv, dkv_other, tail_of(jnp.concatenate([sum_q, sum_kv], axis=0)))
    video_y, short_y = layer_out(core, after(video_result, terms), short_result, wo, wo_other)
    terms, video_y, short_y = lax.optimization_barrier(
        (lax.all_to_all(terms, ("yl", "yh"), 0, 0, tiled=True), video_y, short_y)
    )
    parts = key_parts(terms)
    late, own = scatter((place, second_place), c_turned, x_turned, results, parts)
    grad_kv, bias = key_sum(parts)
    grad_kv, bias, own, *late = lax.optimization_barrier((grad_kv, bias, own, *late))
    grad_out, grad_q = sum((g.astype(F32) for g in late), own)
    return (
        video_y[None],
        short_y[None],
        jnp.concatenate([grad_q, grad_kv], axis=1),
        grad_out.T,
        bias.reshape(768),
    )


def solution(mesh):
    fine = Mesh(mesh.devices.reshape(SIZES), AXES)
    return jax.shard_map(
        per_device,
        mesh=fine,
        in_specs=(
            P(DP, None),
            P(),
            P(DP, None),
            P(DP, GRP, None),
            P(None, DP, GRP),
            P(DP + GRP, None, None),
            P(None, DP + GRP, None),
            P(DP + GRP, None),
            P(DP, GRP, None),
            P(DP + GRP, None, None),
        ),
        out_specs=(
            P(DP, GRP, None),
            P(DP + GRP, None, None),
            P(GRP + DP, None),
            P(None, GRP + DP),
            P(),
        ),
        check_vma=False,
    )
```
